32 devices in a mesh: dp: 16 (over z, x, core), fsdp: 2 (over y).
Axes of the slice: x: 2, y: 2, z: 4, core: 2. Of those that a mesh axis runs over, the one named last changes fastest.
Arguments:
- tokens: bfloat16 [32768, 1024], P(('dp', 'fsdp')), may hold values from -6 to 6
- cotangent: bfloat16 [32768, 1024], P(('dp', 'fsdp')), may hold values from -12 to 12
- item_lengths: int32 [32, 4], P(('dp', 'fsdp')), may hold values from 0 to 1024, as said below
- ln_gain: float32 [1024], P(('dp', 'fsdp')), may hold values from 0.5 to 1.5
- ln_bias: float32 [1024], P(('dp', 'fsdp')), may hold values from -1.75 to 1.75
- w_wide: float32 [1024, 3072], P('dp', 'fsdp'), may hold values from -0.1875 to 0.1875
- bias_wide: float32 [3072], P(('dp', 'fsdp')), may hold values from -1.75 to 1.75
- w_narrow: float32 [1024, 512], P('dp', 'fsdp'), may hold values from -0.1875 to 0.1875
- bias_narrow: float32 [512], P(('dp', 'fsdp')), may hold values from -1.75 to 1.75
- state_mix: float32 [512, 512], P(('dp', 'fsdp')), may hold values from -0.25 to 0.25
- log_rate: float32 [512], P(('dp', 'fsdp')), may hold values from -7 to -2
- w_expand: float32 [512, 3072], P('dp', 'fsdp'), may hold values from -0.5 to 0.5
- bias_expand: float32 [3072], P(('dp', 'fsdp')), may hold values from -1.75 to 1.75
- w_output: float32 [3072, 1024], P('dp', 'fsdp'), may hold values from -0.21875 to 0.21875
- bias_output: float32 [1024], P(('dp', 'fsdp')), may hold values from -1.75 to 1.75
Outputs:
- layer_out: bfloat16 [32768, 1024], P(('dp', 'fsdp'))
- grad_tokens: float32 [32768, 1024], P(('dp', 'fsdp'))
- grad_ln_gain: float32 [1024], P(('dp', 'fsdp'))
- grad_ln_bias: float32 [1024], P(('dp', 'fsdp'))
- grad_w_wide: float32 [1024, 3072], P('dp', 'fsdp')
- grad_bias_wide: float32 [3072], P(('dp', 'fsdp'))
- grad_w_narrow: float32 [1024, 512], P('dp', 'fsdp')
- grad_bias_narrow: float32 [512], P(('dp', 'fsdp'))
- grad_state_mix: float32 [512, 512], P(('dp', 'fsdp'))
- grad_log_rate: float32 [512], P(('dp', 'fsdp'))
- grad_w_expand: float32 [512, 3072], P('dp', 'fsdp')
- grad_bias_expand: float32 [3072], P(('dp', 'fsdp'))
- grad_w_output: float32 [3072, 1024], P('dp', 'fsdp')
- grad_bias_output: float32 [1024], P(('dp', 'fsdp'))
The draws below stay inside these ranges and needn't reach their ends.
Inputs may be any that keep to these rules, and one draw needn't show every extreme that they name: `item_lengths`: each row lists the lengths of the items that make up one device's 1024 rows, in order: multiples of 256 that sum to 1024, nonzero entries first and zeros after. In every draw some device holds a single item of 1024 rows.
All inputs are finite; a program needn't handle non-finite values.
Results may differ from the reference program's by a relative error of at most 0.012.
The reference program's roundings to bfloat16 on the way count: a program that leaves them out, or rounds other values in their place, can miss the bound.
Values may be sent and summed in bfloat16 or wider, within the bound.
A program may use at most 320 MiB of HBM per device.

```python
import jax
import jax.numpy as jnp
from jax import lax

E = 1024
F = 3072
H = 512
N = 512
BLK = 64
ITEMS = 4
TOK_DEV = 1024
SHARDS = 32
TOKENS = 32768


def draw_item_lengths(key, part):
    key = jax.random.fold_in(key, 7)
    patterns = jnp.array([[4, 0, 0, 0], [2, 2, 0, 0], [2, 1, 1, 0], [1, 2, 1, 0], [1, 1, 2, 0], [1, 1, 1, 1]], dtype=jnp.int32)
    pick_key, whole_key = jax.random.split(key)
    picks = jax.random.randint(pick_key, (SHARDS,), 0, 6)
    single = jax.random.randint(whole_key, (), 0, SHARDS)
    picks = jnp.where(jnp.arange(SHARDS) == single, 0, picks)
    return patterns[picks] * (TOK_DEV // 4)


def spiked(result, rng, source, target, shards_of, factor):
    owner, partner = [(jnp.arange(result.shape[axis_at]) // (result.shape[axis_at] // shards_of)).reshape([-1 if axis == axis_at else 1 for axis in range(result.ndim)]) for axis_at in (source, target)]
    chosen = jax.random.permutation(rng, shards_of)[partner]
    strong = (owner == chosen) | (owner == (partner + shards_of // 2) % shards_of)
    return jnp.where(strong, factor * result, result)


def level_of(stream_key, shape, shards, least, high):
    level = 1.0
    for dim, shards_of in shards:
        draws = jax.random.uniform(jax.random.fold_in(jax.random.fold_in(stream_key, 6), dim), (shards_of,), jnp.float32, least / len(shards), high / len(shards))
        level = level * jnp.repeat(jnp.exp(draws), shape[dim] // shards_of).reshape((-1,) + (1,) * (len(shape) - 1 - dim))
    return level


def noise(stream_key, dims, spread, bound, cuts=(), kind=jnp.bfloat16):
    level = level_of(stream_key, dims, cuts, -0.22, 0.18) if cuts else 1.0
    entries = jax.random.normal(stream_key, dims, jnp.float32) * spread * level
    return jnp.minimum(jnp.maximum(entries, -bound), bound).astype(kind)


def bell_draw_with(rng, dims, scale, bound, cuts, heavy, held_as=jnp.bfloat16):
    values = scale * jax.random.normal(rng, dims, jnp.float32)
    if cuts:
        values = values * level_of(rng, dims, cuts, -0.22, 0.18)
    return jnp.clip(spiked(values, jax.random.fold_in(rng, 3), *heavy), -bound, bound).astype(held_as)


def setup_inputs(seed: int = 0) -> dict:
    streams_of = jax.random.split(jax.random.key(seed), 16)
    return {
        "tokens": noise(streams_of[0], (TOKENS, E), 1.0, 6.0, ((0, 32),)),
        "cotangent": bell_draw_with(streams_of[1], (TOKENS, E), 1.0, 12.0, ((0, 32),), (0, 1, 32, 2.75)),
        "item_lengths": draw_item_lengths(jax.random.fold_in(streams_of[15], 71), 0),
        "ln_gain": jnp.clip(1.0 + 0.1 * jax.random.normal(streams_of[3], (E,), jnp.float32), 0.5, 1.5),
        "ln_bias": noise(streams_of[4], (E,), 0.3, 1.75, ((0, 32),), jnp.float32),
        "w_wide": noise(streams_of[5], (E, F), E ** -0.5, 0.1875, ((0, 16), (1, 2)), jnp.float32),
        "bias_wide": noise(streams_of[6], (F,), 0.3, 1.75, ((0, 32),), jnp.float32),
        "w_narrow": noise(streams_of[7], (E, H), E ** -0.5, 0.1875, ((0, 16), (1, 2)), jnp.float32),
        "bias_narrow": noise(streams_of[8], (H,), 0.3, 1.75, ((0, 32),), jnp.float32),
        "state_mix": noise(streams_of[9], (H, N), N ** -0.5, 0.25, ((0, 32),), jnp.float32),
        "log_rate": jnp.clip(-7.0 + 5.0 * jax.random.uniform(streams_of[10], (N,), jnp.float32) ** level_of(streams_of[10], (N,), ((0, 32),), -0.2, 0.2), -7.0, -2.0),
        "w_expand": noise(streams_of[11], (H, F), (H // 4) ** -0.5, 0.5, ((0, 16), (1, 2)), jnp.float32),
        "bias_expand": noise(streams_of[12], (F,), 0.3, 1.75, ((0, 32),), jnp.float32),
        "w_output": noise(streams_of[13], (F, E), (F // 4) ** -0.5, 0.21875, ((0, 16), (1, 2)), jnp.float32),
        "bias_output": noise(streams_of[14], (E,), 0.3, 1.75, ((0, 32),), jnp.float32),
    }


@jax.custom_vjp
def low(v):
    return lax.optimization_barrier(v.astype(jnp.bfloat16)).astype(jnp.float32)

@jax.custom_vjp
def low_back(v):
    return v

def low_keep(v):
    return (low(v), None)

def low_pass(kept, grad):
    return (grad,)

def back_keep(v):
    return (v, None)

def back_low(kept, grad):
    return (low(grad),)
low.defvjp(low_keep, low_pass)
low_back.defvjp(back_keep, back_low)
highest = lax.Precision.HIGHEST
epsilon = 1e-05

def block_keep(lengths, block_count, block_rows):
    starts = jnp.cumsum(lengths, dtype=jnp.int32) - lengths
    firsts = jnp.arange(block_count, dtype=jnp.int32) * block_rows
    begins = (starts[None, :] == firsts[:, None]) & (lengths[None, :] > 0)
    return 1.0 - jnp.any(begins, axis=1).astype(jnp.float32)

def state_space(narrow, state_mix, log_rate, lengths):
    block_rows = BLK
    decay_rates = jnp.exp(log_rate)
    offsets = jnp.arange(block_rows, dtype=jnp.int32)
    places = offsets.astype(jnp.float32)
    input_gain = -jnp.expm1(-decay_rates)
    decay_out = jnp.exp(-decay_rates[None, :] * (places[:, None] + 1.0))
    inject = input_gain[None, :] * jnp.exp(-decay_rates[None, :] * (block_rows - 1.0 - places[:, None]))
    carry_decay = jnp.exp(-decay_rates * block_rows)
    powers = jnp.exp(-decay_rates[:, None] * places[None, :])
    kernel = jnp.dot(state_mix * input_gain[None, :], powers, precision=highest)
    lagged = ((offsets[:, None] - offsets[None, :])[:, :, None] == offsets[None, None, :]).astype(jnp.float32)
    toeplitz = jnp.einsum('hl,tsl->hts', kernel, lagged, precision=highest)
    block_count = narrow.shape[0] // block_rows
    keep_flags = block_keep(lengths, block_count, block_rows)
    blocks = narrow.reshape(block_count, block_rows, narrow.shape[1])
    mix_rows = state_mix.T

    def advance(memory_state, inputs):
        block_in, keep_flag = inputs
        memory_state = memory_state * keep_flag
        inside = jnp.einsum('hts,sh->th', toeplitz, block_in, precision=highest)
        carried = jnp.dot(decay_out, mix_rows * memory_state, precision=highest)
        memory_state = carry_decay[:, None] * memory_state + jnp.dot(inject.T, block_in, precision=highest)
        return (memory_state, inside + carried)
    zero_state = jnp.zeros((state_mix.shape[1], state_mix.shape[0]), jnp.float32)
    last_state, outputs = lax.scan(advance, zero_state, (blocks, keep_flags))
    return outputs.reshape(narrow.shape)

def gss_layer(inputs_f, lengths, params):
    ln_gain, ln_bias, w_wide, bias_wide, w_narrow, bias_narrow, state_mix, log_rate, w_expand, bias_expand, w_output, bias_output = params
    average = lax.optimization_barrier(jnp.mean(inputs_f, axis=-1, keepdims=True))
    centered = inputs_f - average
    variance = lax.optimization_barrier(jnp.mean(centered * centered, axis=-1, keepdims=True))
    normed = centered * lax.rsqrt(variance + epsilon)
    normed_low = low(normed * ln_gain + ln_bias)
    pre_wide = low_back(jnp.dot(normed_low, w_wide, precision=highest) + bias_wide)
    activated = jax.nn.gelu(pre_wide)
    pre_narrow = low_back(jnp.dot(normed_low, w_narrow, precision=highest) + bias_narrow)
    narrow = low(jax.nn.gelu(pre_narrow))
    devices_here = lengths.shape[0]
    scanned = jax.vmap(lambda rows_in, lens_in: state_space(rows_in, state_mix, log_rate, lens_in))(narrow.reshape(devices_here, -1, narrow.shape[1]), lengths).reshape(narrow.shape)
    scanned_low = low(scanned)
    expanded = low_back(jnp.dot(scanned_low, w_expand, precision=highest) + bias_expand)
    gated = low(expanded * activated)
    return jnp.dot(gated, w_output, precision=highest) + bias_output + inputs_f

def reference(tokens, cotangent, item_lengths, ln_gain, ln_bias, w_wide, bias_wide, w_narrow, bias_narrow, state_mix, log_rate, w_expand, bias_expand, w_output, bias_output):
    masters = (ln_gain, ln_bias, w_wide, bias_wide, w_narrow, bias_narrow, state_mix, log_rate, w_expand, bias_expand, w_output, bias_output)
    group_size = 4
    group_count = SHARDS // group_size
    inputs_f = tokens.astype(jnp.float32).reshape(group_count, group_size * TOK_DEV, E)
    grouped_lengths = item_lengths.reshape(group_count, group_size, ITEMS)

    def forward(inputs_all, params):
        rounded = tuple((low(param) for param in params))
        stepper = jax.checkpoint(lambda paired: gss_layer(paired[0], paired[1], rounded))
        return lax.map(stepper, (inputs_all, grouped_lengths))
    outputs, pullback = jax.vjp(forward, inputs_f, masters)
    grad_inputs, grads = pullback(cotangent.astype(jnp.float32).reshape(group_count, group_size * TOK_DEV, E))
    return (outputs.reshape(TOKENS, E).astype(jnp.bfloat16), grad_inputs.reshape(TOKENS, E), grads[0], grads[1], grads[2], grads[3], grads[4], grads[5], grads[6], grads[7], grads[8], grads[9], grads[10], grads[11])
```

```python
import functools

import jax
import jax.numpy as jnp
from jax import lax
from jax.experimental import pallas as pl
from jax.experimental.pallas import tpu as pltpu
from jax.sharding import PartitionSpec as P

BLK = 64
LANES = 128
EPSILON = 1e-05
MESH = pl.DeviceIdType.MESH
BF16 = jnp.bfloat16
F32 = jnp.float32
FIELDS = ("ln_gain", "ln_bias", "bias_wide", "bias_narrow", "log_rate", "bias_expand", "bias_output")

ANY = pl.BlockSpec(memory_space=pl.ANY)
VMEM = pl.BlockSpec(memory_space=pltpu.VMEM)
SMEM = pl.BlockSpec(memory_space=pltpu.SMEM)


def shape_of(*shape, dtype=BF16):
    return jax.ShapeDtypeStruct(shape, dtype)


def nn(a, b):
    return lax.dot_general(a, b, (((1,), (0,)), ((), ())), preferred_element_type=F32)


def nt(a, b):
    return lax.dot_general(a, b, (((1,), (1,)), ((), ())), preferred_element_type=F32)


def tn(a, b):
    return lax.dot_general(a, b, (((0,), (0,)), ((), ())), preferred_element_type=F32)


def split(v):
    high = v.astype(BF16)
    return high, (v - high.astype(F32)).astype(BF16)


def loop(count, body):
    def step(i, carry):
        body(i)
        return carry

    lax.fori_loop(0, count, step, 0)


def span(i, size):
    return pl.ds(pl.multiple_of(i * size, size), size)


def gelu(v):
    root = 0.7978845608028654
    square = v * v
    t = jnp.tanh(v * (root + (root * 0.044715) * square))
    half = 0.5 * (1.0 + t)
    slope = half + (0.5 * v) * (1.0 - t * t) * (root + (3.0 * root * 0.044715) * square)
    return v * half, slope


def owner_mask(devices, length):
    width = length // devices
    device = lax.broadcasted_iota(jnp.int32, (devices, length), 0)
    place = lax.broadcasted_iota(jnp.int32, (devices, length), 1)
    return (place >= device * width) & (place < (device + 1) * width)


def lane_picks(devices, length):
    width = length // devices
    lane = lax.broadcasted_iota(jnp.int32, (LANES, length), 0).astype(F32)
    place = lax.broadcasted_iota(jnp.int32, (LANES, length), 1).astype(F32)
    within = place - width * jnp.floor((place + 0.5) * (1.0 / width))
    return jnp.where(lane == within, 1.0, 0.0).astype(BF16)


def unpack(rows, length):
    devices = rows.shape[0]
    spread = nn(rows, lane_picks(devices, length))
    return jnp.sum(jnp.where(owner_mask(devices, length), spread, 0.0), axis=0, keepdims=True)


def pack(vector, devices):
    length = vector.shape[1]
    high, low = split(jnp.where(owner_mask(devices, length), vector, 0.0))
    picks = lane_picks(devices, length)
    return nt(high, picks) + nt(low, picks)


def scan_tables(rate):
    t = lax.broadcasted_iota(jnp.int32, (BLK, rate.shape[1]), 0).astype(F32)
    decay = jnp.exp(-rate)
    gain = 1.0 - decay
    power = jnp.exp(-rate * t)
    reverse = jnp.exp(-rate * (BLK - 1.0 - t))
    return t, decay, gain, power, reverse, power * decay, gain * reverse


def column(row):
    n = row.shape[1]
    eye = lax.broadcasted_iota(jnp.int32, (n, n), 0) == lax.broadcasted_iota(jnp.int32, (n, n), 1)
    return jnp.sum(jnp.where(eye, row, 0.0), axis=1, keepdims=True)


def make_taps(mix, gain, power, taps):
    high, low = split(gain * power)
    values = nt(high, mix) + nt(low, mix)
    for g in range(taps.shape[0]):
        taps[g, 0:56, :] = jnp.zeros((56, LANES), F32)
        for lag in range(BLK):
            taps[g, (lag + 7) * 8 : (lag + 8) * 8, :] = jnp.broadcast_to(
                values[lag : lag + 1, g * LANES : (g + 1) * LANES], (8, LANES)
            )


def by_place(source, target, blocks):
    def body(j):
        for g in range(source.shape[0]):
            target[g, span(j, blocks), :] = source[g, pl.ds(j, blocks, stride=BLK), :]

    loop(BLK, body)


def eight(i):
    return span(i, 8)


def convolve(taps, source, target, blocks, g):
    halves = blocks // 8

    def tile(out):
        def step(into, totals):
            totals = list(totals)
            ks = [taps[g, eight((out - into) * 8 + m), :] for m in range(15)]
            for i in range(8):
                for half in range(halves):
                    v = source[g, eight((into * 8 + i) * halves + half), :]
                    for o in range(8):
                        totals[o * halves + half] += ks[o - i + 7] * v
            return tuple(totals)

        zero = tuple(jnp.zeros((8, LANES), F32) for _ in range(8 * halves))
        totals = lax.fori_loop(0, out + 1, step, zero)
        for o in range(8):
            for half in range(halves):
                target[g, eight((out * 8 + o) * halves + half), :] = totals[o * halves + half]

    loop(BLK // 8, tile)


def convolve_back(taps, source, target, blocks, g):
    halves = blocks // 8

    def tile(into):
        def step(out, totals):
            totals = list(totals)
            ks = [taps[g, eight((out - into) * 8 + m), :] for m in range(15)]
            for o in range(8):
                for half in range(halves):
                    v = source[g, eight((out * 8 + o) * halves + half), :]
                    for i in range(8):
                        totals[i * halves + half] += ks[o - i + 7] * v
            return tuple(totals)

        zero = tuple(jnp.zeros((8, LANES), F32) for _ in range(8 * halves))
        totals = lax.fori_loop(into, BLK // 8, step, zero)
        for i in range(8):
            for half in range(halves):
                target[g, eight((into * 8 + i) * halves + half), :] = totals[i * halves + half]

    loop(BLK // 8, tile)


def correlate(outs, ins, taps_grad, blocks, g):
    halves = blocks // 8
    taps_grad[g] = jnp.zeros(taps_grad.shape[1:], F32)

    def lag(apart):
        def step(out, totals):
            totals = list(totals)
            into = out - apart
            for half in range(halves):
                us = [ins[g, eight((into * 8 + i) * halves + half), :] for i in range(8)]
                for o in range(8):
                    v = outs[g, eight((out * 8 + o) * halves + half), :]
                    for i in range(8):
                        totals[o - i + 7] += v * us[i]
            return tuple(totals)

        zero = tuple(jnp.zeros((8, LANES), F32) for _ in range(15))
        totals = lax.fori_loop(apart, BLK // 8, step, zero)
        for m in range(15):
            rows = eight(apart * 8 + m)
            taps_grad[g, rows, :] = taps_grad[g, rows, :] + totals[m]

    loop(BLK // 8, lag)


def scan_forward(mix, rate, keep, narrow, narrow4, placed4, conv4, taps, mix_t, carry, state, product, saved, out):
    blocks = narrow.shape[0] // BLK
    _, _, gain, power, _, leave, enter = scan_tables(rate)
    mix_t[...] = mix.astype(F32).T
    make_taps(mix, gain, power, taps)
    carry[...] = jnp.broadcast_to(column(jnp.exp(-rate * BLK)), carry.shape)
    by_place(narrow4, placed4, blocks)
    groups = taps.shape[0]
    loop(groups, lambda g: convolve(taps, placed4, conv4, blocks, g))
    leave = leave.astype(BF16)
    enter = jnp.concatenate(split(enter), axis=0)
    state[...] = jnp.zeros(state.shape, F32)

    def block(b):
        rows = span(b, BLK)
        rows_in = narrow[rows, :]
        twice = jnp.concatenate([rows_in, rows_in], axis=0)
        kept = keep(b)
        for g in range(groups):
            cols = slice(g * LANES, (g + 1) * LANES)
            now = state[:, cols] * kept
            saved[b, :, cols] = now.astype(BF16)
            product[:, cols] = (mix_t[:, cols] * now).astype(BF16)
            state[:, cols] = carry[...] * now + tn(enter, twice[:, cols])
        carried = nn(leave, product[...])
        for g in range(groups):
            cols = slice(g * LANES, (g + 1) * LANES)
            inside = conv4[g, pl.ds(b, BLK, stride=blocks), :]
            out[rows, cols] = (carried[:, cols] + inside).astype(BF16)

    loop(blocks, block)


def scan_backward(
    mix, rate, keep, narrow, placed4, d_out, d_out4, d_placed4, conv4, taps, taps_grad, mix_t, carry,
    adjoint, adjoint_low, product, mix_grad_t, overlap, saved, d_narrow,
):
    blocks = narrow.shape[0] // BLK
    t, decay, gain, power, reverse, leave, enter = scan_tables(rate)
    by_place(d_out4, d_placed4, blocks)
    groups = taps.shape[0]
    loop(groups, lambda g: convolve_back(taps, d_placed4, conv4, blocks, g))
    loop(groups, lambda g: correlate(d_placed4, placed4, taps_grad, blocks, g))
    leave_slope = -(t + 1.0) * leave
    enter_slope = decay * reverse - (BLK - 1.0 - t) * enter
    tap_slope = decay * power - t * gain * power
    leave, enter = leave.astype(BF16), enter.astype(BF16)
    adjoint[...] = jnp.zeros(adjoint.shape, F32)
    mix_grad_t[...] = jnp.zeros(mix_grad_t.shape, F32)
    overlap[...] = jnp.zeros(overlap.shape, F32)

    def block(i, total):
        b = blocks - 1 - i
        rows = span(b, BLK)
        rows_in, rows_out = narrow[rows, :], d_out[rows, :]
        kept = keep(b)
        for g in range(groups):
            cols = slice(g * LANES, (g + 1) * LANES)
            state = saved[b, :, cols].astype(F32)
            after = adjoint[:, cols]
            coefficients = mix_t[:, cols]
            reach = tn(leave, rows_out[:, cols])
            adjoint_low[:, cols] = after.astype(BF16)
            product[:, cols] = (coefficients * state).astype(BF16)
            overlap[...] += after * state
            mix_grad_t[:, cols] += state * reach
            adjoint[:, cols] = kept * (coefficients * reach + carry[...] * after)
        entered = nn(enter, adjoint_low[...])
        for g in range(groups):
            cols = slice(g * LANES, (g + 1) * LANES)
            d_narrow[rows, cols] = entered[:, cols] + conv4[g, pl.ds(b, BLK, stride=blocks), :]
        return total + enter_slope * nt(rows_in, adjoint_low[...]) + leave_slope * nt(rows_out, product[...])

    total = lax.fori_loop(0, blocks, block, jnp.zeros((BLK, rate.shape[1]), F32))
    lags = jnp.concatenate(
        [jnp.sum(taps_grad[g].reshape(BLK + 8, 8, LANES), axis=1)[7 : 7 + BLK, :] for g in range(groups)], axis=1
    )
    lags_high, lags_low = split(lags)
    powers_high, powers_low = split(gain * power)
    mix_grad_t[...] += tn(
        jnp.concatenate([powers_high, powers_low, powers_high], axis=0),
        jnp.concatenate([lags_high, lags_high, lags_low], axis=0),
    )
    total = total + tap_slope * (nn(lags_high, mix) + nn(lags_low, mix))
    ones = jnp.ones((8, LANES), BF16)
    high, low = split(overlap[...])
    overlaps = (nt(ones, high) + nt(ones, low))[0:1, :]
    total = jnp.sum(total, axis=0, keepdims=True) - float(BLK) * jnp.exp(-rate * BLK) * overlaps
    return rate * total


def whole(ref, y, cols=slice(None)):
    part = ref[:, :, :, y, :, cols]
    return part.reshape(-1, part.shape[-1])


def normalise(rows):
    rows = rows.astype(F32)
    centered = rows - jnp.mean(rows, axis=-1, keepdims=True)
    variance = jnp.mean(centered * centered, axis=-1, keepdims=True)
    inverse = lax.rsqrt(variance + EPSILON)
    return centered * inverse, inverse


def front_kernel(
    keep, tokens, misc, w_narrow,
    fields_out, normed_low, narrow, slope, scanned, saved, placed4, taps, mix_t, carry,
    narrow4, conv4, state, product,
):
    devices = misc.shape[0] * misc.shape[1] * misc.shape[2] * misc.shape[3]
    n = misc.shape[5]
    mix_rows = n // devices
    block = misc[...].reshape(devices, misc.shape[4], n)
    mix = block[:, 0:mix_rows, :].reshape(n, n)
    rows = block[:, mix_rows : mix_rows + 16, 0:LANES].astype(F32)
    row = 0
    fields = []
    lengths = [f.shape[1] for f in fields_out]
    for f, length in enumerate(lengths):
        vector = unpack(rows[:, f, :].astype(BF16), length)
        fields_out[f][...] = vector
    gain, bias, bias_narrow, rate_log = fields_out[0][...], fields_out[1][...], fields_out[3][...], fields_out[4][...]

    def norm(i):
        rows = span(i, 128)
        normed, _ = normalise(tokens[rows, :])
        normed_low[rows, :] = (normed * gain + bias).astype(BF16)

    loop(tokens.shape[0] // 128, norm)
    half = bias_narrow.shape[1] // 2
    for y in range(2):
        cols = slice(y * half, (y + 1) * half)
        weights = whole(w_narrow, y)

        def project(i):
            rows = span(i, 256)
            value, grad = gelu(nn(normed_low[rows, :], weights) + bias_narrow[:, cols])
            low = value.astype(BF16)
            narrow[rows, cols] = low
            slope[rows, cols] = grad.astype(BF16)
            for g in range(half // LANES):
                narrow4[y * (half // LANES) + g, rows, :] = low[:, g * LANES : (g + 1) * LANES].astype(F32)

        loop(tokens.shape[0] // 256, project)
    scan_forward(
        mix, jnp.exp(rate_log), lambda b: keep[b], narrow, narrow4, placed4, conv4, taps, mix_t, carry, state, product,
        saved, scanned,
    )


def middle_kernel(
    tokens, cotangent, normed_low, scanned, w_wide, w_expand, w_output, bias_wide, bias_expand, bias_output,
    activated, steep, layer_out, grad_output, gated,
):
    half = w_wide.shape[5]
    tile = 512
    for y in range(2):

        def widen(j):
            cols = span(j, tile)
            full = pl.ds(pl.multiple_of(y * half + j * tile, tile), tile)
            expanded = nn(scanned[...], whole(w_expand, y, cols)) + bias_expand[:, full]
            value, slope = gelu(nn(normed_low[...], whole(w_wide, y, cols)) + bias_wide[:, full])
            activated[:, full] = value.astype(BF16)
            steep[:, full] = (expanded * slope).astype(BF16)
            gated[:, full] = (expanded * value).astype(BF16)

        loop(half // tile, widen)
    half = w_output.shape[5]
    for y in range(2):
        cols = slice(y * half, (y + 1) * half)

        def project(i):
            rows = span(i, 512)
            total = nn(gated[rows, :], whole(w_output, y)) + bias_output[:, cols]
            layer_out[rows, cols] = (total + tokens[rows, cols].astype(F32)).astype(BF16)

        loop(tokens.shape[0] // 512, project)
    layers = grad_output.shape[0]
    slab = gated.shape[1] // layers

    def weigh(z):
        rows = pl.ds(pl.multiple_of(z * slab, 128), slab)
        for y in range(2):
            part = tn(gated[:, rows], cotangent[:, y * half : (y + 1) * half])
            grad_output[z, :, :, y] = part.astype(BF16).reshape(grad_output.shape[1:3] + grad_output.shape[4:])

    loop(layers, weigh)


def sums(v):
    return jnp.sum(v.astype(F32), axis=0, keepdims=True)


def back_kernel(
    cotangent, normed_low, scanned, w_output, w_expand, activated, steep,
    d_pre_wide, d_scanned, d_scanned4, grad_expand, grad_wide, sum_wide, sum_expand, sum_output,
    d_expanded,
):
    layers = w_output.shape[0]
    slab = activated.shape[1] // layers
    half = w_output.shape[5]

    def gate(z):
        cols = pl.ds(pl.multiple_of(z * slab, 128), slab)
        rows = w_output[z].reshape(2, 2, 2, -1, half)
        d_gated = sum(
            nt(cotangent[:, y * half : (y + 1) * half], rows[:, :, y].reshape(slab, half)) for y in range(2)
        )
        low = (d_gated * activated[:, cols].astype(F32)).astype(BF16)
        d_expanded[:, cols] = low
        sum_expand[:, cols] = sums(low)
        low = (d_gated * steep[:, cols].astype(F32)).astype(BF16)
        d_pre_wide[:, cols] = low
        sum_wide[:, cols] = sums(low)

    loop(layers, gate)
    sum_output[...] = sums(cotangent[...])
    half = w_expand.shape[5]
    for h in range(2):
        lanes = d_scanned.shape[1] // 2
        part = sum(
            nt(
                d_expanded[:, y * half : (y + 1) * half],
                w_expand[h * layers // 2 : (h + 1) * layers // 2, :, :, y].reshape(lanes, half),
            )
            for y in range(2)
        )
        d_scanned[:, h * lanes : (h + 1) * lanes] = part.astype(BF16)
        for g in range(lanes // LANES):
            d_scanned4[h * (lanes // LANES) + g] = part[:, g * LANES : (g + 1) * LANES]
    tile = 512
    for y in range(2):

        def weigh(j):
            cols = span(j, tile)
            full = pl.ds(pl.multiple_of(y * half + j * tile, tile), tile)
            shape = grad_expand.shape[0:3] + (grad_expand.shape[4], tile)
            grad_expand[:, :, :, y, :, cols] = tn(scanned[...], d_expanded[:, full]).astype(BF16).reshape(shape)
            shape = grad_wide.shape[0:3] + (grad_wide.shape[4], tile)
            grad_wide[:, :, :, y, :, cols] = tn(normed_low[...], d_pre_wide[:, full]).astype(BF16).reshape(shape)

        loop(half // tile, weigh)


def scan_kernel(
    keep, misc, rate_log, narrow, placed4, slope, normed_low, d_scanned, d_scanned4, taps, mix_t, carry, saved,
    d_pre_narrow, grad_narrow, mix_grad_t, grad_rate, sum_narrow,
    d_placed4, conv4, taps_grad, adjoint, adjoint_low, product, overlap, d_narrow,
):
    devices = misc.shape[0] * misc.shape[1] * misc.shape[2] * misc.shape[3]
    n = misc.shape[5]
    mix = misc[...].reshape(devices, misc.shape[4], n)[:, 0 : n // devices, :].reshape(n, n)
    grad_rate[...] = scan_backward(
        mix, jnp.exp(rate_log[...]), lambda b: keep[b], narrow, placed4, d_scanned, d_scanned4, d_placed4, conv4,
        taps, taps_grad, mix_t, carry, adjoint, adjoint_low, product, mix_grad_t, overlap, saved, d_narrow,
    )
    low = (d_narrow[...] * slope[...].astype(F32)).astype(BF16)
    d_pre_narrow[...] = low
    sum_narrow[...] = sums(low)
    half = grad_narrow.shape[5]
    for y in range(2):
        shape = grad_narrow.shape[0:3] + grad_narrow.shape[4:]
        part = tn(normed_low[...], d_pre_narrow[:, y * half : (y + 1) * half])
        grad_narrow[:, :, :, y] = part.astype(BF16).reshape(shape)


def end_kernel(
    tokens, cotangent, gain, d_pre_wide, d_pre_narrow, w_wide, w_narrow, mix_grad_t, *rest
):
    sums_in, (grad_tokens, misc_grad, sum_gain, sum_bias) = rest[:-4], rest[-4:]
    sum_gain[...] = jnp.zeros(sum_gain.shape, F32)
    sum_bias[...] = jnp.zeros(sum_bias.shape, F32)
    wide, narrow = w_wide.shape[5], w_narrow.shape[5]

    def norm(i):
        rows = span(i, 256)
        d_normed = sum(
            nt(d_pre_wide[rows, y * wide : (y + 1) * wide], whole(w_wide, y))
            + nt(d_pre_narrow[rows, y * narrow : (y + 1) * narrow], whole(w_narrow, y))
            for y in range(2)
        )
        normed, inverse = normalise(tokens[rows, :])
        sum_gain[...] += sums(d_normed * normed)
        sum_bias[...] += sums(d_normed)
        scaled = d_normed * gain[...]
        inner = scaled - jnp.mean(scaled, axis=-1, keepdims=True)
        inner = inner - normed * jnp.mean(scaled * normed, axis=-1, keepdims=True)
        grad_tokens[rows, :] = cotangent[rows, :].astype(F32) + inverse * inner

    loop(tokens.shape[0] // 256, norm)
    devices = misc_grad.shape[0]
    n = misc_grad.shape[2]
    mix_rows = n // devices
    misc_grad[:, 0:mix_rows, :] = mix_grad_t[...].T.reshape(devices, mix_rows, n).astype(BF16)
    vectors = [sum_gain[...], sum_bias[...]] + [v[...] for v in sums_in]
    packed = [pack(v, devices)[:, None, :] for v in vectors]
    packed.append(jnp.zeros((devices, 16 - len(packed), LANES), F32))
    misc_grad[:, mix_rows : mix_rows + 16, 0:LANES] = jnp.concatenate(packed, axis=1).astype(BF16)
    misc_grad[:, mix_rows : mix_rows + 16, LANES:n] = jnp.zeros((devices, 16, n - LANES), BF16)


def place():
    dp = lax.axis_index("dp")
    return dp // 4, (dp // 2) % 2, dp % 2, lax.axis_index("fsdp")


def device(z, x, c, y):
    return (z * 4 + x * 2 + c, y)


def greet(layers):
    z, x, c, y = place()
    barrier = pltpu.get_barrier_semaphore()
    peers = [device((z + k) % layers, x, c, y) for k in range(1, layers)]
    peers += [device(z, 1 - x, c, y), device(z, x, c, 1 - y), device(z, x, 1 - c, y)]
    for peer in peers:
        pl.semaphore_signal(barrier, inc=1, device_id=peer, device_id_type=MESH)
    pl.semaphore_wait(barrier, len(peers))


def remote(source, target, send, recv, peer):
    return pltpu.make_async_remote_copy(
        src_ref=source, dst_ref=target, send_sem=send, recv_sem=recv, device_id=peer, device_id_type=MESH
    )


def start(copies):
    for copy in copies:
        copy.start()


def wait_recv(copies):
    for copy in copies:
        copy.wait_recv()


def wait_send(copies):
    for copy in copies:
        copy.wait_send()


class Gather:
    def __init__(self, full, rows, cols, send, recv):
        z, x, c, y = place()
        layers = full.shape[0]
        low, count = rows
        half = count // 2
        a, b, both = pl.ds(low, half), pl.ds(low + half, half), pl.ds(low, count)
        k, zs, two = pl.ds(*cols), pl.ds(0, layers), pl.ds(0, 2)

        def copy(ref, n, peer):
            return remote(ref, ref, send.at[n], recv.at[n], peer)

        n = layers - 1
        to_x, to_y, to_c = device(z, 1 - x, c, y), device(z, x, c, 1 - y), device(z, x, 1 - c, y)
        self.along = lambda: [
            copy(full.at[z, x, c, y, both, k], i - 1, device((z + i) % layers, x, c, y)) for i in range(1, layers)
        ]
        self.first = lambda: [
            copy(full.at[zs, x, c, y, a, k], n, to_x),
            copy(full.at[zs, x, c, y, b, k], n + 1, to_y),
        ]
        self.second = lambda: [
            copy(full.at[zs, two, c, y, a, k], n + 2, to_y),
            copy(full.at[zs, x, c, two, b, k], n + 3, to_x),
        ]
        self.across = [
            lambda: [copy(full.at[zs, x, c, y, both, k], n + 4, to_c)],
            lambda: [
                copy(full.at[zs, 1 - x, c, y, a, k], n + 5, to_c),
                copy(full.at[zs, x, c, 1 - y, b, k], n + 6, to_c),
            ],
            lambda: [
                copy(full.at[zs, two, c, 1 - y, a, k], n + 7, to_c),
                copy(full.at[zs, 1 - x, c, two, b, k], n + 8, to_c),
            ],
        ]


def gather_steps(parts):
    count = len(parts)
    start(parts[0].along())
    start(parts[1].along())
    for s in range(count + 3):
        if s < count:
            wait_recv(parts[s].along())
            start(parts[s].first())
            if s + 2 < count:
                start(parts[s + 2].along())
        if 0 <= s - 1 < count:
            wait_recv(parts[s - 1].first())
            start(parts[s - 1].second())
        if s < count:
            start(parts[s].across[0]())
        if 0 <= s - 1 < count:
            start(parts[s - 1].across[1]())
        if 0 <= s - 2 < count:
            wait_recv(parts[s - 2].second())
            start(parts[s - 2].across[2]())
        if 0 <= s - 3 < count:
            for step in parts[s - 3].across:
                wait_recv(step())
        yield
    for part in parts:
        for step in (part.along, part.first, part.second, *part.across):
            wait_send(step())


def cut(shards):
    _, narrow, expand, wide, output = (s[-2:] for s in shards)
    parts = [(1, (0, narrow[0]), (0, narrow[1]))]
    tile = 512
    parts += [(2, (0, expand[0]), (j, tile)) for j in range(0, expand[1], tile)]
    parts += [(3, (i, 32), (j, tile)) for j in range(0, wide[1], tile) for i in range(0, wide[0], 32)]
    parts += [(4, (i, 32), (0, output[1])) for i in range(0, output[0], 32)]
    return parts


def gather_kernel(parts, *refs):
    count = (len(refs) - 2) // 2
    shards, fulls, (send, recv) = refs[:count], refs[count : 2 * count], refs[2 * count :]
    z, x, c, y = place()
    for shard, full in zip(shards, fulls):
        full[z, x, c, y] = shard[...].astype(BF16)
    greet(fulls[0].shape[0])
    moves = [Gather(fulls[i], rows, cols, send.at[k], recv.at[k]) for k, (i, rows, cols) in enumerate(parts)]
    for _ in gather_steps(moves):
        pass


def gather(shards, layers):
    parts = [(0, (0, shards[0].shape[0]), (0, shards[0].shape[1]))] + cut([s.shape for s in shards])
    count = len(shards)
    return pl.pallas_call(
        functools.partial(gather_kernel, parts),
        out_shape=[shape_of(layers, 2, 2, 2, *s.shape) for s in shards],
        in_specs=[VMEM] * count,
        out_specs=[VMEM] * count,
        scratch_shapes=[pltpu.SemaphoreType.DMA((len(parts), layers + 8))] * 2,
        compiler_params=pltpu.CompilerParams(collective_id=0, has_side_effects=True, vmem_limit_bytes=48 << 20),
    )(*shards)


class Scatter:
    def __init__(self, buffers, send, recv):
        self.kept, self.got, self.a1, self.b1, self.a2, self.b2, self.gz = buffers
        kept = self.kept
        z, x, c, y = self.at = place()
        layers = self.layers = kept.shape[0]
        half = self.half = kept.shape[3] // 2
        a, b = pl.ds(0, half), pl.ds(half, half)
        zs, two = pl.ds(0, layers), pl.ds(0, 2)
        to_x, to_y, to_c = device(z, 1 - x, c, y), device(z, x, c, 1 - y), device(z, x, 1 - c, y)

        def copy(source, target, n, peer):
            return remote(source, target, send.at[n], recv.at[n], peer)

        self.across = lambda source: copy(source, self.got, 0, to_c)
        self.first_a = lambda: copy(kept.at[zs, two, 1 - y, a], self.a1, 1, to_y)
        self.first_b = lambda: copy(kept.at[zs, 1 - x, two, b], self.b1, 2, to_x)
        self.second_a = lambda: copy(kept.at[zs, 1 - x, y, a], self.a2, 3, to_x)
        self.second_b = lambda: copy(kept.at[zs, x, 1 - y, b], self.b2, 4, to_y)
        self.along = lambda: [
            copy(kept.at[(z + i) % layers, x, y], self.gz.at[i - 1], 4 + i, device((z + i) % layers, x, c, y))
            for i in range(1, layers)
        ]

    def add(self, where, got):
        self.kept[where] = (self.kept[where].astype(F32) + got.astype(F32)).astype(BF16)

    def add_across(self):
        z, x, c, y = self.at
        every, a, b = slice(None), slice(0, self.half), slice(self.half, 2 * self.half)

        def add(*where):
            self.add(where, self.got[where])

        add(every, every, 1 - y, a)
        self.first_a().start()
        add(every, 1 - x, every, b)
        self.first_b().start()
        add(every, every, y, a)
        add(every, x, every, b)

    def add_first(self):
        z, x, c, y = self.at
        every, a, b = slice(None), slice(0, self.half), slice(self.half, 2 * self.half)
        self.first_a().wait_recv()
        self.first_a().wait_send()
        self.add((every, 1 - x, y, a), self.a1[:, 1 - x])
        self.second_a().start()
        self.first_b().wait_recv()
        self.first_b().wait_send()
        self.add((every, x, 1 - y, b), self.b1[:, 1 - y])
        self.second_b().start()
        self.add((every, x, y, a), self.a1[:, x])
        self.add((every, x, y, b), self.b1[:, y])

    def add_second(self):
        z, x, c, y = self.at
        every, a, b = slice(None), slice(0, self.half), slice(self.half, 2 * self.half)
        self.second_a().wait_recv()
        self.add((every, x, y, a), self.a2[...])
        self.second_b().wait_recv()
        self.add((every, x, y, b), self.b2[...])
        start(self.along())

    def total(self):
        z, x, c, y = self.at
        wait_recv(self.along())
        value = self.kept[z, x, y].astype(F32)
        for i in range(self.layers - 1):
            value = value + self.gz[i].astype(F32)
        return value

    def drain(self):
        wait_send([self.second_a(), self.second_b(), *self.along()])


def scatter_buffers(rows, cols, layers):
    half = rows // 2
    shapes = [(layers, 2, 2, rows, cols)] * 2 + [(layers, 2, half, cols)] * 2
    shapes += [(layers, half, cols)] * 2 + [(layers - 1, rows, cols)]
    return [pltpu.VMEM(s, BF16) for s in shapes]


def scatter_kernel(parts, count, *refs):
    fulls, outs, rest = refs[:count], refs[count : 2 * count], refs[2 * count :]
    send, recv, local = rest[-3:]
    z, x, c, y = place()
    layers = fulls[0].shape[0]
    total = len(parts)
    moves = [Scatter(rest[7 * k : 7 * k + 7], send.at[k], recv.at[k]) for k in range(total)]

    def source(k, core):
        i, rows, cols = parts[k]
        return fulls[i].at[pl.ds(0, layers), pl.ds(0, 2), core, pl.ds(0, 2), pl.ds(*rows), pl.ds(*cols)]

    greet(layers)
    mine = [pltpu.make_async_copy(source(k, c), moves[k].kept, local.at[k]) for k in range(total)]
    for k in range(total):
        mine[k].start()
        moves[k].across(source(k, 1 - c)).start()
    for s in range(total + 3):
        if s < total:
            mine[s].wait()
            moves[s].across(source(s, 1 - c)).wait_recv()
            moves[s].add_across()
        if 0 <= s - 1 < total:
            moves[s - 1].add_first()
        if 0 <= s - 2 < total:
            moves[s - 2].add_second()
        if 0 <= s - 3 < total:
            i, (row, rows), (col, cols) = parts[s - 3]
            outs[i][row : row + rows, col : col + cols] = moves[s - 3].total()
    for k in range(total):
        moves[k].across(source(k, 1 - c)).wait_send()
        moves[k].drain()


def scatter(fulls, layers):
    shards = [f.shape[4:] for f in fulls]
    parts = cut(shards)
    parts = parts[-(shards[4][0] // 32) :] + parts[1 : -(shards[4][0] // 32)] + parts[:1]
    parts.append((0, (0, shards[0][0]), (0, shards[0][1])))
    count = len(fulls)
    buffers = [b for _, rows, cols in parts for b in scatter_buffers(rows[1], cols[1], layers)]
    width = 4 + layers
    return pl.pallas_call(
        functools.partial(scatter_kernel, parts, count),
        out_shape=[shape_of(*s, dtype=F32) for s in shards],
        in_specs=[ANY] * count,
        out_specs=[VMEM] * count,
        scratch_shapes=buffers + [pltpu.SemaphoreType.DMA((len(parts), width))] * 2 + [pltpu.SemaphoreType.DMA((len(parts),))],
        compiler_params=pltpu.CompilerParams(collective_id=1, has_side_effects=True, vmem_limit_bytes=48 << 20),
    )(*fulls)


def call(kernel, outs, ins, scratch=(), in_specs=None):
    return pl.pallas_call(
        kernel,
        out_shape=outs,
        in_specs=in_specs or [VMEM] * len(ins),
        out_specs=jax.tree.map(lambda _: VMEM, outs),
        scratch_shapes=list(scratch),
        compiler_params=pltpu.CompilerParams(vmem_limit_bytes=58 << 20),
    )(*ins)


def layer(tokens, cotangent, item_lengths, fulls, lengths):
    misc, w_narrow, w_expand, w_wide, w_output = fulls
    t, e = tokens.shape
    n = misc.shape[5]
    h = n
    f = lengths[2]
    blocks, groups = t // BLK, h // LANES
    tap_rows = (BLK + 8) * 8
    ends = jnp.cumsum(item_lengths[0])
    firsts = jnp.arange(blocks, dtype=jnp.int32) * BLK
    begins = jnp.any((ends - item_lengths[0])[None, :] == firsts[:, None], axis=1)
    keep = 1.0 - begins.astype(F32)
    by_lane = lambda: shape_of(groups, t, LANES, dtype=F32)
    scratch4 = pltpu.VMEM((groups, t, LANES), F32)
    square = pltpu.VMEM((n, h), F32)
    square_low = pltpu.VMEM((n, h), BF16)
    fields, normed_low, narrow, slope, scanned, saved, placed4, taps, mix_t, carry = call(
        front_kernel,
        [
            [shape_of(1, length, dtype=F32) for length in lengths],
            shape_of(t, e), shape_of(t, h), shape_of(t, h), shape_of(t, h), shape_of(blocks, n, h),
            by_lane(), shape_of(groups, tap_rows, LANES, dtype=F32), shape_of(n, h, dtype=F32),
            shape_of(n, LANES, dtype=F32),
        ],
        (keep, tokens, misc, w_narrow),
        [scratch4, scratch4, square, square_low],
        [SMEM, VMEM, VMEM, VMEM],
    )
    gain, _, bias_wide, _, rate_log, bias_expand, bias_output = fields
    activated, steep, layer_out, grad_output = call(
        middle_kernel,
        [shape_of(t, f), shape_of(t, f), shape_of(t, e), shape_of(*w_output.shape)],
        (tokens, cotangent, normed_low, scanned, w_wide, w_expand, w_output, bias_wide, bias_expand, bias_output),
        [pltpu.VMEM((t, f), BF16)],
    )
    row = lambda k: shape_of(1, k, dtype=F32)
    d_pre_wide, d_scanned, d_scanned4, grad_expand, grad_wide, sum_wide, sum_expand, sum_output = call(
        back_kernel,
        [shape_of(t, f), shape_of(t, h), by_lane(), shape_of(*w_expand.shape), shape_of(*w_wide.shape), row(f), row(f), row(e)],
        (cotangent, normed_low, scanned, w_output, w_expand, activated, steep),
        [pltpu.VMEM((t, f), BF16)],
    )
    ins = (keep, misc, rate_log, narrow, placed4, slope, normed_low, d_scanned, d_scanned4, taps, mix_t, carry, saved)
    d_pre_narrow, grad_narrow, mix_grad_t, grad_rate, sum_narrow = call(
        scan_kernel,
        [shape_of(t, h), shape_of(*w_narrow.shape), shape_of(n, h, dtype=F32), row(n), row(h)],
        ins,
        [
            scratch4, scratch4, pltpu.VMEM((groups, tap_rows, LANES), F32), square, square_low, square_low,
            pltpu.VMEM((n, LANES), F32), pltpu.VMEM((t, h), F32),
        ],
        [SMEM] + [VMEM] * (len(ins) - 1),
    )
    devices = misc.shape[0] * 8
    grad_tokens, misc_grad = call(
        end_kernel,
        [shape_of(t, e, dtype=F32), shape_of(devices, misc.shape[4], n)],
        (tokens, cotangent, gain, d_pre_wide, d_pre_narrow, w_wide, w_narrow, mix_grad_t,
         sum_wide, sum_narrow, grad_rate, sum_expand, sum_output),
        [pltpu.VMEM((1, e), F32)] * 2,
    )
    misc_grad = misc_grad.reshape(misc.shape)
    return layer_out, grad_tokens, [misc_grad, grad_narrow, grad_expand, grad_wide, grad_output]


VIRTUAL = 4


def block_rows(state_mix, vectors, devices):
    n = state_mix.shape[1]
    rows = [jnp.pad(v.astype(BF16).reshape(devices, 1, -1), ((0, 0), (0, 0), (0, n - v.shape[0] // devices))) for v in vectors]
    rows.append(jnp.zeros((devices, 16 - len(rows), n), BF16))
    return jnp.concatenate([state_mix.astype(BF16).reshape(devices, -1, n)] + rows, axis=1)


def to_blocks(matrix):
    rows, cols = matrix.shape
    return matrix.reshape(VIRTUAL, 2, 2, rows // (4 * VIRTUAL), 2, cols // 2).transpose(0, 1, 2, 4, 3, 5)


def from_blocks(blocks):
    layers, _, _, _, rows, cols = blocks.shape
    return blocks.transpose(0, 1, 2, 4, 3, 5).reshape(layers * 4 * rows, 2 * cols)


def collect(state_mix, vectors, matrices):
    every = ("dp", "fsdp")

    def whole_of(v):
        return lax.all_gather(v.astype(BF16), every, axis=0, tiled=True)

    misc = block_rows(whole_of(state_mix), [whole_of(v) for v in vectors], 8 * VIRTUAL)
    misc = misc.reshape((VIRTUAL, 2, 2, 2) + misc.shape[1:])
    fulls = []
    for m in matrices:
        m = lax.all_gather(m.astype(BF16), "dp", axis=0, tiled=True)
        fulls.append(to_blocks(lax.all_gather(m, "fsdp", axis=1, tiled=True)))
    return [misc] + fulls


def spread(grads, lengths):
    every = ("dp", "fsdp")
    misc, *matrices = grads
    misc = misc.reshape((8 * VIRTUAL,) + misc.shape[4:]).astype(F32)
    n = misc.shape[2]
    mix_rows = n // (8 * VIRTUAL)
    small = [misc[:, :mix_rows].reshape(n, n)]
    small += [misc[:, mix_rows + i, : length // (8 * VIRTUAL)].reshape(length) for i, length in enumerate(lengths)]
    small = [lax.psum_scatter(v, every, scatter_dimension=0, tiled=True) for v in small]
    outs = []
    for m in matrices:
        m = lax.psum_scatter(from_blocks(m).astype(F32), "dp", scatter_dimension=0, tiled=True)
        outs.append(lax.psum_scatter(m, "fsdp", scatter_dimension=1, tiled=True))
    return small[0], small[1:], outs


def fits(dp, fsdp, state_mix, matrices):
    whole_tiles = all(m.shape[0] % 32 == 0 and m.shape[1] % LANES == 0 for m in matrices)
    return dp % 4 == 0 and dp > 4 and fsdp == 2 and state_mix.shape[0] % 16 == 0 and whole_tiles


def shards(
    dp, fsdp, tokens, cotangent, item_lengths, ln_gain, ln_bias, w_wide, bias_wide, w_narrow, bias_narrow, state_mix,
    log_rate, w_expand, bias_expand, w_output, bias_output,
):
    vectors = (ln_gain, ln_bias, bias_wide, bias_narrow, log_rate, bias_expand, bias_output)
    matrices = (w_narrow, w_expand, w_wide, w_output)
    lengths = [v.shape[0] * dp * fsdp for v in vectors]
    if fits(dp, fsdp, state_mix, matrices):
        fulls = gather([block_rows(state_mix, vectors, 1)[0], *matrices], dp // 4)
        layer_out, grad_tokens, grads = layer(tokens, cotangent, item_lengths, fulls, lengths)
        misc_grad, *matrix_grads = scatter(grads, dp // 4)
        mix_rows = state_mix.shape[0]
        mix_grad = misc_grad[:mix_rows]
        vector_grads = [misc_grad[mix_rows + i, : v.shape[0]] for i, v in enumerate(vectors)]
    else:
        fulls = collect(state_mix, vectors, matrices)
        layer_out, grad_tokens, grads = layer(tokens, cotangent, item_lengths, fulls, lengths)
        mix_grad, vector_grads, matrix_grads = spread(grads, lengths)
    gain_grad, shift_grad, wide_bias_grad, narrow_bias_grad, rate_grad, expand_bias_grad, output_bias_grad = vector_grads
    narrow_grad, expand_grad, wide_grad, output_grad = matrix_grads
    return (
        layer_out, grad_tokens, gain_grad, shift_grad, wide_grad, wide_bias_grad, narrow_grad, narrow_bias_grad,
        mix_grad, rate_grad, expand_grad, expand_bias_grad, output_grad, output_bias_grad,
    )


def solution(mesh):
    every = ("dp", "fsdp")
    matrix, vector, rows = P("dp", "fsdp"), P(every), P(every, None)
    return jax.shard_map(
        functools.partial(shards, mesh.shape["dp"], mesh.shape["fsdp"]),
        mesh=mesh,
        in_specs=(
            rows, rows, rows, vector, vector, matrix, vector, matrix, vector, rows, vector, matrix, vector, matrix, vector,
        ),
        out_specs=(
            rows, rows, vector, vector, matrix, vector, matrix, vector, rows, vector, matrix, vector, matrix, vector,
        ),
        check_vma=False,
    )
```

```python
import functools

import jax
import jax.numpy as jnp
from jax import lax
from jax.experimental import pallas as pl
from jax.experimental.pallas import tpu as pltpu
from jax.sharding import PartitionSpec as P

BLK = 64
LANES = 128
TILE = 512
PACE_FORWARD = 3.0
PACE_BACKWARD = 4.0
EPSILON = 1e-05
MESH = pl.DeviceIdType.MESH
BF16 = jnp.bfloat16
F32 = jnp.float32
FIELDS = ("ln_gain", "ln_bias", "bias_wide", "bias_narrow", "log_rate", "bias_expand", "bias_output")

ANY = pl.BlockSpec(memory_space=pl.ANY)
VMEM = pl.BlockSpec(memory_space=pltpu.VMEM)
SMEM = pl.BlockSpec(memory_space=pltpu.SMEM)


def shape_of(*shape, dtype=BF16):
    return jax.ShapeDtypeStruct(shape, dtype)


def nn(a, b):
    return lax.dot_general(a, b, (((1,), (0,)), ((), ())), preferred_element_type=F32)


def nt(a, b):
    return lax.dot_general(a, b, (((1,), (1,)), ((), ())), preferred_element_type=F32)


def tn(a, b):
    return lax.dot_general(a, b, (((0,), (0,)), ((), ())), preferred_element_type=F32)


def split(v):
    high = v.astype(BF16)
    return high, (v - high.astype(F32)).astype(BF16)


def loop(count, body):
    def step(i, carry):
        body(i)
        return carry

    lax.fori_loop(0, count, step, 0)


def span(i, size):
    return pl.ds(pl.multiple_of(i * size, size), size)


def gelu(v):
    root = 0.7978845608028654
    square = v * v
    t = jnp.tanh(v * (root + (root * 0.044715) * square))
    half = 0.5 * (1.0 + t)
    slope = half + (0.5 * v) * (1.0 - t * t) * (root + (3.0 * root * 0.044715) * square)
    return v * half, slope


def owner_mask(devices, length):
    width = length // devices
    device = lax.broadcasted_iota(jnp.int32, (devices, length), 0)
    place = lax.broadcasted_iota(jnp.int32, (devices, length), 1)
    return (place >= device * width) & (place < (device + 1) * width)


def lane_picks(devices, length):
    width = length // devices
    lane = lax.broadcasted_iota(jnp.int32, (LANES, length), 0).astype(F32)
    place = lax.broadcasted_iota(jnp.int32, (LANES, length), 1).astype(F32)
    within = place - width * jnp.floor((place + 0.5) * (1.0 / width))
    return jnp.where(lane == within, 1.0, 0.0).astype(BF16)


def unpack(rows, length):
    devices = rows.shape[0]
    spread = nn(rows, lane_picks(devices, length))
    return jnp.sum(jnp.where(owner_mask(devices, length), spread, 0.0), axis=0, keepdims=True)


def pack(vector, devices):
    length = vector.shape[1]
    high, low = split(jnp.where(owner_mask(devices, length), vector, 0.0))
    picks = lane_picks(devices, length)
    return nt(high, picks) + nt(low, picks)


def scan_tables(rate):
    t = lax.broadcasted_iota(jnp.int32, (BLK, rate.shape[1]), 0).astype(F32)
    decay = jnp.exp(-rate)
    gain = 1.0 - decay
    power = jnp.exp(-rate * t)
    reverse = jnp.exp(-rate * (BLK - 1.0 - t))
    return t, decay, gain, power, reverse, power * decay, gain * reverse


def column(row):
    n = row.shape[1]
    eye = lax.broadcasted_iota(jnp.int32, (n, n), 0) == lax.broadcasted_iota(jnp.int32, (n, n), 1)
    return jnp.sum(jnp.where(eye, row, 0.0), axis=1, keepdims=True)


def make_taps(mix, gain, power, taps):
    high, low = split(gain * power)
    values = nt(high, mix) + nt(low, mix)
    for g in range(taps.shape[0]):
        taps[g, 0:56, :] = jnp.zeros((56, LANES), F32)
        for lag in range(BLK):
            taps[g, (lag + 7) * 8 : (lag + 8) * 8, :] = jnp.broadcast_to(
                values[lag : lag + 1, g * LANES : (g + 1) * LANES], (8, LANES)
            )


def by_place(source, target, blocks):
    def body(j):
        for g in range(source.shape[0]):
            target[g, span(j, blocks), :] = source[g, pl.ds(j, blocks, stride=BLK), :]

    loop(BLK, body)


def eight(i):
    return span(i, 8)


def convolve(taps, source, target, blocks, g):
    halves = blocks // 8

    def tile(out):
        def step(into, totals):
            totals = list(totals)
            ks = [taps[g, eight((out - into) * 8 + m), :] for m in range(15)]
            for i in range(8):
                for half in range(halves):
                    v = source[g, eight((into * 8 + i) * halves + half), :]
                    for o in range(8):
                        totals[o * halves + half] += ks[o - i + 7] * v
            return tuple(totals)

        zero = tuple(jnp.zeros((8, LANES), F32) for _ in range(8 * halves))
        totals = lax.fori_loop(0, out + 1, step, zero)
        for o in range(8):
            for half in range(halves):
                target[g, eight((out * 8 + o) * halves + half), :] = totals[o * halves + half]

    loop(BLK // 8, tile)


def convolve_back(taps, source, target, blocks, g):
    halves = blocks // 8

    def tile(into):
        def step(out, totals):
            totals = list(totals)
            ks = [taps[g, eight((out - into) * 8 + m), :] for m in range(15)]
            for o in range(8):
                for half in range(halves):
                    v = source[g, eight((out * 8 + o) * halves + half), :]
                    for i in range(8):
                        totals[i * halves + half] += ks[o - i + 7] * v
            return tuple(totals)

        zero = tuple(jnp.zeros((8, LANES), F32) for _ in range(8 * halves))
        totals = lax.fori_loop(into, BLK // 8, step, zero)
        for i in range(8):
            for half in range(halves):
                target[g, eight((into * 8 + i) * halves + half), :] = totals[i * halves + half]

    loop(BLK // 8, tile)


def correlate(outs, ins, taps_grad, blocks, g):
    halves = blocks // 8
    taps_grad[g] = jnp.zeros(taps_grad.shape[1:], F32)

    def lag(apart):
        def step(out, totals):
            totals = list(totals)
            into = out - apart
            for half in range(halves):
                us = [ins[g, eight((into * 8 + i) * halves + half), :] for i in range(8)]
                for o in range(8):
                    v = outs[g, eight((out * 8 + o) * halves + half), :]
                    for i in range(8):
                        totals[o - i + 7] += v * us[i]
            return tuple(totals)

        zero = tuple(jnp.zeros((8, LANES), F32) for _ in range(15))
        totals = lax.fori_loop(apart, BLK // 8, step, zero)
        for m in range(15):
            rows = eight(apart * 8 + m)
            taps_grad[g, rows, :] = taps_grad[g, rows, :] + totals[m]

    loop(BLK // 8, lag)


def convolve_back_flat(taps, source, target, blocks, g):
    halves = blocks // 8
    for into in range(BLK // 8):
        totals = [None] * (8 * halves)
        for out in range(into, BLK // 8):
            lowest = 7 if out == into else 0
            ks = {m: taps[g, eight((out - into) * 8 + m), :] for m in range(lowest, 15)}
            for half in range(halves):
                for o in range(8):
                    v = source[g, eight((out * 8 + o) * halves + half), :]
                    for i in range(8):
                        if o - i + 7 >= lowest:
                            at, term = i * halves + half, ks[o - i + 7] * v
                            totals[at] = term if totals[at] is None else totals[at] + term
        for i in range(8):
            for half in range(halves):
                target[g, eight((into * 8 + i) * halves + half), :] = totals[i * halves + half]


def correlate_flat(outs, ins, taps_grad, blocks, g):
    halves = blocks // 8
    for apart in range(BLK // 8):
        totals = [None] * 15
        for out in range(apart, BLK // 8):
            into = out - apart
            for half in range(halves):
                us = [ins[g, eight((into * 8 + i) * halves + half), :] for i in range(8)]
                for o in range(8):
                    v = outs[g, eight((out * 8 + o) * halves + half), :]
                    for i in range(8):
                        m = o - i + 7
                        if apart or m >= 7:
                            totals[m] = v * us[i] if totals[m] is None else totals[m] + v * us[i]
        for m in range(7, 15):
            taps_grad[g, eight(apart * 8 + m), :] = totals[m]
        for m in range(7):
            if apart:
                rows = eight(apart * 8 + m)
                taps_grad[g, rows, :] = taps_grad[g, rows, :] + totals[m]


def scan_prepare(mix, rate, taps, mix_t, carry):
    _, _, gain, power, _, _, _ = scan_tables(rate)
    mix_t[...] = mix.astype(F32).T
    make_taps(mix, gain, power, taps)
    carry[...] = jnp.broadcast_to(column(jnp.exp(-rate * BLK)), carry.shape)


def scan_forward(rate, keep, narrow, narrow4, placed4, conv4, taps, mix_t, carry, state, product, enter_t, save, saved, out, tick):
    blocks = narrow.shape[0] // BLK
    _, _, _, _, _, leave, enter = scan_tables(rate)
    by_place(narrow4, placed4, blocks)
    groups = taps.shape[0]
    for g in range(groups):
        convolve(taps, placed4, conv4, blocks, g)
        tick(1.5)
    leave = leave.astype(BF16)
    enter_t[...] = jnp.concatenate(split(enter), axis=0).T
    state[...] = jnp.zeros(state.shape, F32)

    def block(b):
        rows = span(b, BLK)
        rows_in = narrow[rows, :]
        twice = jnp.concatenate([rows_in, rows_in], axis=0)
        kept = keep(b)
        slot = save(b)
        for g in range(state.shape[0] // LANES):
            some = slice(g * LANES, (g + 1) * LANES)
            now = state[some, :] * kept
            slot[some, :] = now.astype(BF16)
            product[some, :] = (mix_t[some, :] * now).astype(BF16)
            state[some, :] = jnp.concatenate([carry[some, :]] * groups, axis=1) * now + nn(enter_t[some, :], twice)
        saved(b)
        carried = nn(leave, product[...])
        for g in range(groups):
            cols = slice(g * LANES, (g + 1) * LANES)
            inside = conv4[g, pl.ds(b, BLK, stride=blocks), :]
            out[rows, cols] = (carried[:, cols] + inside).astype(BF16)

    quarter = blocks // 4
    for q in range(4):
        loop(quarter, lambda i: block(q * quarter + i))
        tick(1.8)


def scan_backward(
    mix, rate, keep, narrow, placed4, d_out, d_out4, d_placed4, conv4, taps, taps_grad, mix_t, carry,
    adjoint, adjoint_low, product, leave_t, mix_grad_t, overlap, load, d_narrow, tick, convolved=False,
):
    blocks = narrow.shape[0] // BLK
    t, decay, gain, power, reverse, leave, enter = scan_tables(rate)
    groups = conv4.shape[0]
    if not convolved:
        by_place(d_out4, d_placed4, blocks)
        for g in range(groups):
            convolve_back(taps, d_placed4, conv4, blocks, g)
        for g in range(groups):
            correlate(d_placed4, placed4, taps_grad, blocks, g)
    leave_slope = -(t + 1.0) * leave
    enter_slope = decay * reverse - (BLK - 1.0 - t) * enter
    tap_slope = decay * power - t * gain * power
    leave_t[...] = leave.astype(BF16).T
    enter = enter.astype(BF16)
    adjoint[...] = jnp.zeros(adjoint.shape, F32)
    mix_grad_t[...] = jnp.zeros(mix_grad_t.shape, F32)
    overlap[...] = jnp.zeros(overlap.shape, F32)

    def block(i, total):
        b = blocks - 1 - i
        rows = span(b, BLK)
        rows_in, rows_out = narrow[rows, :], d_out[rows, :]
        kept = keep(b)
        saved = load(b)
        for g in range(adjoint.shape[0] // LANES):
            some = slice(g * LANES, (g + 1) * LANES)
            state = saved[some, :].astype(F32)
            after = adjoint[some, :]
            coefficients = mix_t[some, :]
            reach = nn(leave_t[some, :], rows_out)
            adjoint_low[some, :] = after.astype(BF16)
            product[some, :] = (coefficients * state).astype(BF16)
            met = after * state
            overlap[some, :] += sum(met[:, k * LANES : (k + 1) * LANES] for k in range(groups))
            mix_grad_t[some, :] += state * reach
            decays = jnp.concatenate([carry[some, :]] * groups, axis=1)
            adjoint[some, :] = kept * (coefficients * reach + decays * after)
        entered = nn(enter, adjoint_low[...])
        for g in range(groups):
            cols = slice(g * LANES, (g + 1) * LANES)
            d_narrow[rows, cols] = entered[:, cols] + conv4[g, pl.ds(b, BLK, stride=blocks), :]
        return total + enter_slope * nt(rows_in, adjoint_low[...]) + leave_slope * nt(rows_out, product[...])

    total = jnp.zeros((BLK, rate.shape[1]), F32)
    quarter = blocks // 4
    for q in range(4):
        total = lax.fori_loop(q * quarter, (q + 1) * quarter, block, total)
        tick(3.5)
    lags = jnp.concatenate(
        [jnp.sum(taps_grad[g].reshape(BLK + 8, 8, LANES), axis=1)[7 : 7 + BLK, :] for g in range(groups)], axis=1
    )
    lags_high, lags_low = split(lags)
    powers_high, powers_low = split(gain * power)
    mix_grad_t[...] += tn(
        jnp.concatenate([powers_high, powers_low, powers_high], axis=0),
        jnp.concatenate([lags_high, lags_high, lags_low], axis=0),
    )
    total = total + tap_slope * (nn(lags_high, mix) + nn(lags_low, mix))
    ones = jnp.ones((8, LANES), BF16)
    high, low = split(overlap[...])
    overlaps = (nt(ones, high) + nt(ones, low))[0:1, :]
    total = jnp.sum(total, axis=0, keepdims=True) - float(BLK) * jnp.exp(-rate * BLK) * overlaps
    return rate * total


def whole(ref, y, cols=slice(None)):
    part = ref[:, :, :, y, :, cols]
    return part.reshape(-1, part.shape[-1])


def normalise(rows):
    rows = rows.astype(F32)
    centered = rows - jnp.mean(rows, axis=-1, keepdims=True)
    variance = jnp.mean(centered * centered, axis=-1, keepdims=True)
    inverse = lax.rsqrt(variance + EPSILON)
    return centered * inverse, inverse


def forward_kernel(parts, keep, tokens, cotangent, weights, outs, scratch):
    (
        mix_out, fields_out, normed_low_out, narrow_out, slope_out, scanned_out, saved_out, placed4_out, taps_out,
        mix_t_out, carry_out, activated_out, steep_out, gated_out, grad_output_out, *fulls_out,
    ) = outs
    (
        normed_low, narrow, slope, scanned, wide4, taps, mix_t, carry, state, product, enter_t, saved, activated, steep,
        gated, stage, sems, saved_sems, tile_sems, stage_sems, *comm,
    ) = scratch
    pending = []

    def publish(source, target):
        copy = pltpu.make_async_copy(source, target, sems.at[len(pending)])
        copy.start()
        pending.append(copy)

    rows_all = tokens.shape[0]
    groups = tokens.shape[1] // LANES

    def norm(i):
        rows = span(i, 128)
        normed, _ = normalise(tokens[rows, :])
        for g in range(groups):
            wide4[g, rows, :] = normed[:, g * LANES : (g + 1) * LANES]

    def normalise_rows():
        loop(rows_all // 128, norm)

    if parts is None:
        normalise_rows()
        fulls, comm = weights, Progress(None, PACE_FORWARD)
    else:
        *fulls, send, recv = comm
        z, x, c, y = place()
        call_peers(fulls[0].shape[0])
        for shard, full in zip(weights[1:5], fulls[1:]):
            full[z, x, c, y] = shard[...].astype(BF16)
        mix_part, vectors = weights[0], weights[5:]
        mix_rows = mix_part.shape[0]
        state[0:16, :] = jnp.zeros((16, state.shape[1]), F32)
        for f, vector in enumerate(vectors):
            state[f : f + 1, 0 : vector.shape[1]] = vector[...]
        fulls[0][z, x, c, y, 0:mix_rows, :] = mix_part[...].astype(BF16)
        fulls[0][z, x, c, y, mix_rows : mix_rows + 16, :] = state[0:16, :].astype(BF16)
        normalise_rows()
        hear_peers(fulls[0].shape[0])
        moves = [Gather(fulls[i], rows, cols, send.at[k], recv.at[k]) for k, (i, rows, cols) in enumerate(parts)]
        comm = Progress(gather_steps(moves), PACE_FORWARD)

    def arrived(array, col=None):
        if parts is not None:
            comm.until(ready(parts, array, col))

    misc, w_narrow, w_expand, w_wide, w_output = fulls
    arrived(0)
    devices = misc.shape[0] * misc.shape[1] * misc.shape[2] * misc.shape[3]
    n = misc.shape[5]
    mix_rows = n // devices
    block = misc[...].reshape(devices, misc.shape[4], n)
    mix = block[:, 0:mix_rows, :].reshape(n, n)
    mix_out[...] = mix
    rows = block[:, mix_rows : mix_rows + 16, 0:LANES].astype(F32)
    for f, field in enumerate(fields_out):
        field[...] = unpack(rows[:, f, :].astype(BF16), field.shape[1])
    gain, bias, bias_wide, bias_narrow, rate_log, bias_expand, bias_output = (f[...] for f in fields_out)
    rate = jnp.exp(rate_log)

    def shift(i):
        rows = span(i, 128)
        for g in range(groups):
            cols = slice(g * LANES, (g + 1) * LANES)
            normed_low[rows, cols] = (wide4[g, rows, :] * gain[:, cols] + bias[:, cols]).astype(BF16)

    loop(rows_all // 128, shift)
    publish(normed_low, normed_low_out)
    scan_prepare(mix, rate, taps, mix_t, carry)
    publish(taps, taps_out)
    publish(mix_t, mix_t_out)
    publish(carry, carry_out)
    arrived(1)
    scan_groups = n // LANES
    placed4, conv4, narrow4 = (wide4.at[pl.ds(k * scan_groups, scan_groups)] for k in range(3))
    half = bias_narrow.shape[1] // 2
    for y in range(2):
        cols = slice(y * half, (y + 1) * half)

        def project(i):
            rows = span(i, 512)
            value, grad = gelu(nn(normed_low[rows, :], whole(w_narrow, y)) + bias_narrow[:, cols])
            low = value.astype(BF16)
            narrow[rows, cols] = low
            slope[rows, cols] = grad.astype(BF16)
            for g in range(half // LANES):
                narrow4[y * (half // LANES) + g, rows, :] = low[:, g * LANES : (g + 1) * LANES].astype(F32)

        loop(rows_all // 512, project)
        comm.spend(0.8)
    publish(narrow, narrow_out)
    publish(slope, slope_out)

    def saving(b):
        return pltpu.make_async_copy(saved.at[b % 2], saved_out.at[b], saved_sems.at[b % 2])

    def save(b):
        @pl.when(b >= 2)
        def _():
            saving(b - 2).wait()

        return saved.at[b % 2]

    blocks = rows_all // BLK
    quarter = blocks // 4
    scan_forward(
        rate, lambda b: keep[b], narrow, narrow4, placed4, conv4, taps, mix_t, carry, state, product, enter_t, save,
        lambda b: saving(b).start(), scanned, comm.spend,
    )
    saving(blocks - 2).wait()
    saving(blocks - 1).wait()
    publish(placed4, placed4_out)
    publish(scanned, scanned_out)
    if parts is not None:
        arrived(2)
        publish(w_narrow, fulls_out[0])
        publish(w_expand, fulls_out[1])
    half = w_wide.shape[5]
    flushes = []
    for j in range(half // TILE):
        arrived(3, j * TILE)
        for y in range(2):
            slot = (2 * j + y) % 2
            if 2 * j + y >= 2:
                for flush in flushes[2 * j + y - 2]:
                    flush.wait()
            cols = slice(j * TILE, (j + 1) * TILE)
            full = slice(y * half + j * TILE, y * half + (j + 1) * TILE)
            some = rows_all // 2

            def widen(i):
                rows = span(i, some)
                expanded = nn(scanned[rows, :], whole(w_expand, y, cols)) + bias_expand[:, full]
                value, grad = gelu(nn(normed_low[rows, :], whole(w_wide, y, cols)) + bias_wide[:, full])
                activated[slot, rows, :] = value.astype(BF16)
                steep[slot, rows, :] = (expanded * grad).astype(BF16)
                gated[rows, full] = (expanded * value).astype(BF16)

            loop(2, widen)
            flushes.append([
                pltpu.make_async_copy(activated.at[slot], activated_out.at[:, full], tile_sems.at[slot, 0]),
                pltpu.make_async_copy(steep.at[slot], steep_out.at[:, full], tile_sems.at[slot, 1]),
            ])
            start(flushes[-1])
            comm.spend(3.0)
    for pair in flushes[-2:]:
        for flush in pair:
            flush.wait()
    if parts is not None:
        publish(w_wide, fulls_out[2])
    publish(gated, gated_out)
    layers = w_output.shape[0]
    half = w_output.shape[5]
    slab = gated.shape[1] // layers
    flushes = []
    for z_ in range(layers):
        slot = z_ % 2
        if z_ >= 2:
            flushes[z_ - 2].wait()
        for y_ in range(2):
            part = tn(gated[:, z_ * slab : (z_ + 1) * slab], cotangent[:, y_ * half : (y_ + 1) * half])
            stage[slot, :, :, y_] = part.astype(BF16).reshape(2, 2, slab // 4, half)
        flushes.append(pltpu.make_async_copy(stage.at[slot], grad_output_out.at[z_], stage_sems.at[slot]))
        flushes[-1].start()
        comm.spend(2.4)
    for flush in flushes[-2:]:
        flush.wait()
    if parts is not None:
        arrived(4)
        publish(w_output, fulls_out[3])
    if parts is not None:
        comm.until(whole_at(len(parts) - 1) + 1)
    for copy in pending:
        copy.wait()


def forward(keep, tokens, cotangent, weights, lengths, shapes, parts):
    t, e = tokens.shape
    n = shapes[0][5]
    f = lengths[2]
    blocks, groups, layers = t // BLK, n // LANES, shapes[4][0]
    tap_rows = (BLK + 8) * 8
    wide = lambda *s: shape_of(*s, dtype=F32)
    outs = [
        shape_of(n, n), [wide(1, length) for length in lengths], shape_of(t, e), shape_of(t, n), shape_of(t, n),
        shape_of(t, n), shape_of(blocks, n, n), wide(groups, t, LANES), wide(groups, tap_rows, LANES), wide(n, n),
        wide(n, LANES), shape_of(t, f), shape_of(t, f), shape_of(t, f), shape_of(*shapes[4]),
    ]
    specs = [VMEM, [VMEM] * len(lengths)] + [ANY] * 13
    stage = (2,) + tuple(shapes[4][1:])
    scratch = [
        pltpu.VMEM((t, e), BF16), pltpu.VMEM((t, n), BF16), pltpu.VMEM((t, n), BF16), pltpu.VMEM((t, n), BF16),
        pltpu.VMEM((max(3 * groups, e // LANES), t, LANES), F32), pltpu.VMEM((groups, tap_rows, LANES), F32),
        pltpu.VMEM((n, n), F32), pltpu.VMEM((n, LANES), F32), pltpu.VMEM((n, n), F32), pltpu.VMEM((n, n), BF16),
        pltpu.VMEM((n, 2 * BLK), BF16), pltpu.VMEM((2, n, n), BF16), pltpu.VMEM((2, t, TILE), BF16),
        pltpu.VMEM((2, t, TILE), BF16), pltpu.VMEM((t, f), BF16), pltpu.VMEM(stage, BF16),
        pltpu.SemaphoreType.DMA((16,)), pltpu.SemaphoreType.DMA((2,)), pltpu.SemaphoreType.DMA((2, 2)),
        pltpu.SemaphoreType.DMA((2,)),
    ]
    params = dict(vmem_limit_bytes=60 << 20)
    if parts is not None:
        outs += [shape_of(*s) for s in shapes[1:]]
        specs += [ANY] * 4
        scratch += [pltpu.VMEM(s, BF16) for s in shapes]
        scratch += [pltpu.SemaphoreType.DMA((len(parts), layers + 8))] * 2
        params.update(collective_id=0, has_side_effects=True)

    def kernel(*refs):
        ins, rest = refs[: 3 + len(weights)], refs[3 + len(weights) :]
        forward_kernel(parts, *ins[:3], ins[3:], rest[: len(outs)], rest[len(outs) :])

    return pl.pallas_call(
        kernel,
        out_shape=outs,
        in_specs=[SMEM] + [VMEM] * (2 + len(weights)),
        out_specs=specs,
        scratch_shapes=scratch,
        compiler_params=pltpu.CompilerParams(**params),
    )(keep, tokens, cotangent, *weights)


def sums(v):
    return jnp.sum(v.astype(F32), axis=0, keepdims=True)


def back_kernel(
    cotangent, normed_low, scanned, w_output, w_expand, activated, steep,
    d_pre_wide, d_scanned, d_scanned4, grad_expand, grad_wide, sum_wide, sum_expand, sum_output,
    d_expanded,
):
    layers = w_output.shape[0]
    slab = activated.shape[1] // layers
    half = w_output.shape[5]

    def gate(z):
        cols = pl.ds(pl.multiple_of(z * slab, 128), slab)
        rows = w_output[z].reshape(2, 2, 2, -1, half)
        d_gated = sum(
            nt(cotangent[:, y * half : (y + 1) * half], rows[:, :, y].reshape(slab, half)) for y in range(2)
        )
        low = (d_gated * activated[:, cols].astype(F32)).astype(BF16)
        d_expanded[:, cols] = low
        sum_expand[:, cols] = sums(low)
        low = (d_gated * steep[:, cols].astype(F32)).astype(BF16)
        d_pre_wide[:, cols] = low
        sum_wide[:, cols] = sums(low)

    loop(layers, gate)
    sum_output[...] = sums(cotangent[...])
    half = w_expand.shape[5]
    for h in range(2):
        lanes = d_scanned.shape[1] // 2
        part = sum(
            nt(
                d_expanded[:, y * half : (y + 1) * half],
                w_expand[h * layers // 2 : (h + 1) * layers // 2, :, :, y].reshape(lanes, half),
            )
            for y in range(2)
        )
        d_scanned[:, h * lanes : (h + 1) * lanes] = part.astype(BF16)
        for g in range(lanes // LANES):
            d_scanned4[h * (lanes // LANES) + g] = part[:, g * LANES : (g + 1) * LANES]
    tile = 512
    for y in range(2):

        def weigh(j):
            cols = span(j, tile)
            full = pl.ds(pl.multiple_of(y * half + j * tile, tile), tile)
            shape = grad_expand.shape[0:3] + (grad_expand.shape[4], tile)
            grad_expand[:, :, :, y, :, cols] = tn(scanned[...], d_expanded[:, full]).astype(BF16).reshape(shape)
            shape = grad_wide.shape[0:3] + (grad_wide.shape[4], tile)
            grad_wide[:, :, :, y, :, cols] = tn(normed_low[...], d_pre_wide[:, full]).astype(BF16).reshape(shape)

        loop(half // tile, weigh)


def scan_kernel(
    keep, mix, rate_log, narrow, placed4, slope, normed_low, d_scanned, d_scanned4, taps, mix_t, carry, saved,
    d_pre_narrow, grad_narrow, mix_grad_t, grad_rate, sum_narrow,
    d_placed4, conv4, taps_grad, adjoint, adjoint_low, product, overlap, d_narrow, leave_t,
):
    grad_rate[...] = scan_backward(
        mix[...], jnp.exp(rate_log[...]), lambda b: keep[b], narrow, placed4, d_scanned, d_scanned4, d_placed4, conv4,
        taps, taps_grad, mix_t, carry, adjoint, adjoint_low, product, leave_t, mix_grad_t, overlap,
        lambda b: saved.at[b], d_narrow, lambda us: None,
    )
    low = (d_narrow[...] * slope[...].astype(F32)).astype(BF16)
    d_pre_narrow[...] = low
    sum_narrow[...] = sums(low)
    half = grad_narrow.shape[5]
    for y in range(2):
        shape = grad_narrow.shape[0:3] + grad_narrow.shape[4:]
        part = tn(normed_low[...], d_pre_narrow[:, y * half : (y + 1) * half])
        grad_narrow[:, :, :, y] = part.astype(BF16).reshape(shape)


def end_kernel(
    tokens, cotangent, gain, d_pre_wide, d_pre_narrow, w_wide, w_narrow, mix_grad_t, *rest
):
    sums_in, (grad_tokens, misc_grad, sum_gain, sum_bias) = rest[:-4], rest[-4:]
    sum_gain[...] = jnp.zeros(sum_gain.shape, F32)
    sum_bias[...] = jnp.zeros(sum_bias.shape, F32)
    wide, narrow = w_wide.shape[5], w_narrow.shape[5]

    def norm(i):
        rows = span(i, 256)
        d_normed = sum(
            nt(d_pre_wide[rows, y * wide : (y + 1) * wide], whole(w_wide, y))
            + nt(d_pre_narrow[rows, y * narrow : (y + 1) * narrow], whole(w_narrow, y))
            for y in range(2)
        )
        normed, inverse = normalise(tokens[rows, :])
        sum_gain[...] += sums(d_normed * normed)
        sum_bias[...] += sums(d_normed)
        scaled = d_normed * gain[...]
        inner = scaled - jnp.mean(scaled, axis=-1, keepdims=True)
        inner = inner - normed * jnp.mean(scaled * normed, axis=-1, keepdims=True)
        grad_tokens[rows, :] = cotangent[rows, :].astype(F32) + inverse * inner

    loop(tokens.shape[0] // 256, norm)
    devices = misc_grad.shape[0]
    n = misc_grad.shape[2]
    mix_rows = n // devices
    misc_grad[:, 0:mix_rows, :] = mix_grad_t[...].T.reshape(devices, mix_rows, n).astype(BF16)
    vectors = [sum_gain[...], sum_bias[...]] + [v[...] for v in sums_in]
    packed = [pack(v, devices)[:, None, :] for v in vectors]
    packed.append(jnp.zeros((devices, 16 - len(packed), LANES), F32))
    misc_grad[:, mix_rows : mix_rows + 16, 0:LANES] = jnp.concatenate(packed, axis=1).astype(BF16)
    misc_grad[:, mix_rows : mix_rows + 16, LANES:n] = jnp.zeros((devices, 16, n - LANES), BF16)


def place():
    dp = lax.axis_index("dp")
    return dp // 4, (dp // 2) % 2, dp % 2, lax.axis_index("fsdp")


def device(z, x, c, y):
    return (z * 4 + x * 2 + c, y)


def peers_of(layers):
    z, x, c, y = place()
    peers = [device((z + k) % layers, x, c, y) for k in range(1, layers)]
    return peers + [device(z, 1 - x, c, y), device(z, x, c, 1 - y), device(z, x, 1 - c, y)]


def call_peers(layers):
    barrier = pltpu.get_barrier_semaphore()
    for peer in peers_of(layers):
        pl.semaphore_signal(barrier, inc=1, device_id=peer, device_id_type=MESH)


def hear_peers(layers):
    pl.semaphore_wait(pltpu.get_barrier_semaphore(), layers + 2)


def remote(source, target, send, recv, peer):
    return pltpu.make_async_remote_copy(
        src_ref=source, dst_ref=target, send_sem=send, recv_sem=recv, device_id=peer, device_id_type=MESH
    )


def start(copies):
    for copy in copies:
        copy.start()


def wait_recv(copies):
    for copy in copies:
        copy.wait_recv()


def wait_send(copies):
    for copy in copies:
        copy.wait_send()


class Gather:
    def __init__(self, full, rows, cols, send, recv):
        z, x, c, y = place()
        layers = full.shape[0]
        low, count = rows
        half = count // 2
        a, b, both = pl.ds(low, half), pl.ds(low + half, half), pl.ds(low, count)
        k, zs, two = pl.ds(*cols), pl.ds(0, layers), pl.ds(0, 2)

        def copy(ref, n, peer):
            return remote(ref, ref, send.at[n], recv.at[n], peer)

        n = layers - 1
        to_x, to_y, to_c = device(z, 1 - x, c, y), device(z, x, c, 1 - y), device(z, x, 1 - c, y)
        self.along = lambda: [
            copy(full.at[z, x, c, y, both, k], i - 1, device((z + i) % layers, x, c, y)) for i in range(1, layers)
        ]
        self.first = lambda: [
            copy(full.at[zs, x, c, y, a, k], n, to_x),
            copy(full.at[zs, x, c, y, b, k], n + 1, to_y),
        ]
        self.second = lambda: [
            copy(full.at[zs, two, c, y, a, k], n + 2, to_y),
            copy(full.at[zs, x, c, two, b, k], n + 3, to_x),
        ]
        self.across = [
            lambda: [copy(full.at[zs, x, c, y, both, k], n + 4, to_c)],
            lambda: [
                copy(full.at[zs, 1 - x, c, y, a, k], n + 5, to_c),
                copy(full.at[zs, x, c, 1 - y, b, k], n + 6, to_c),
            ],
            lambda: [
                copy(full.at[zs, two, c, 1 - y, a, k], n + 7, to_c),
                copy(full.at[zs, 1 - x, c, two, b, k], n + 8, to_c),
            ],
        ]


def gather_steps(parts):
    count = len(parts)
    ahead = 3
    for part in parts[:ahead]:
        start(part.along())
    yield

    def due(step, stage):
        return [p for p in range(count) if p + 1 + stage * (EARLY if p < 2 else LATE) == step]

    for step in range(1, whole_at(count - 1) + 1):
        for p in due(step, 0):
            wait_recv(parts[p].along())
            start(parts[p].first())
            if p + ahead < count:
                start(parts[p + ahead].along())
        for p in due(step, 1):
            wait_recv(parts[p].first())
            start(parts[p].second())
            start(parts[p].across[0]())
            start(parts[p].across[1]())
        for p in due(step, 2):
            wait_recv(parts[p].second())
            start(parts[p].across[2]())
        for p in range(count):
            if whole_at(p) == step:
                for copies in parts[p].across:
                    wait_recv(copies())
        yield
    for part in parts:
        for step in (part.along, part.first, part.second, *part.across):
            wait_send(step())


EARLY, LATE = 1, 2


def whole_at(part):
    return part + 2 + 2 * (EARLY if part < 2 else LATE)


class Progress:
    def __init__(self, steps, pace):
        self.steps, self.done, self.pace, self.left = steps, 0, pace, pace
        if steps is not None:
            next(steps)

    def step(self):
        if self.steps is not None:
            next(self.steps, None)
        self.done += 1
        self.left = self.pace

    def until(self, count):
        while self.done < count:
            self.step()

    def spend(self, us, limit=None):
        self.left -= us
        while self.left <= 0:
            if limit is not None and self.done >= limit:
                self.left = 0.0
                return
            over = self.left
            self.step()
            self.left += over


def gather_parts(shards):
    misc, narrow, expand, wide, output = shards
    parts = [(0, (0, misc[0]), (0, misc[1])), (1, (0, narrow[0]), (0, narrow[1]))]
    parts += [(2, (0, expand[0]), (j, TILE)) for j in range(0, expand[1], TILE)]
    parts += [(3, (i, 32), (j, TILE)) for j in range(0, wide[1], TILE) for i in range(0, wide[0], 32)]
    parts += [(4, (i, 32), (0, output[1])) for i in range(0, output[0], 32)]
    return parts


def ready(parts, array, col=None):
    wanted = [k for k, (i, _, cols) in enumerate(parts) if i == array and (col is None or cols[0] <= col)]
    return whole_at(wanted[-1])


def scatter_parts(shards):
    misc, narrow, expand, wide, output = shards
    parts = [(4, (i, 32), (0, output[1])) for i in range(0, output[0], 32)]
    parts += [(2, (0, expand[0]), (j, TILE)) for j in range(0, expand[1], TILE)]
    parts += [(3, (i, 32), (j, TILE)) for j in range(0, wide[1], TILE) for i in range(0, wide[0], 32)]
    parts += [(1, (0, narrow[0]), (0, narrow[1])), (0, (0, misc[0]), (0, misc[1]))]
    return parts


class Scatter:
    def __init__(self, buffers, send, recv):
        self.kept, self.got, self.a1, self.b1, self.a2, self.b2, self.gz = buffers
        kept = self.kept
        z, x, c, y = self.at = place()
        layers = self.layers = kept.shape[0]
        half = self.half = kept.shape[3] // 2
        a, b = pl.ds(0, half), pl.ds(half, half)
        zs, two = pl.ds(0, layers), pl.ds(0, 2)
        to_x, to_y, to_c = device(z, 1 - x, c, y), device(z, x, c, 1 - y), device(z, x, 1 - c, y)

        def copy(source, target, n, peer):
            return remote(source, target, send.at[n], recv.at[n], peer)

        self.across = lambda source: copy(source, self.got, 0, to_c)
        self.first_a = lambda: copy(kept.at[zs, two, 1 - y, a], self.a1, 1, to_y)
        self.first_b = lambda: copy(kept.at[zs, 1 - x, two, b], self.b1, 2, to_x)
        self.second_a = lambda: copy(kept.at[zs, 1 - x, y, a], self.a2, 3, to_x)
        self.second_b = lambda: copy(kept.at[zs, x, 1 - y, b], self.b2, 4, to_y)
        self.along = lambda: [
            copy(kept.at[(z + i) % layers, x, y], self.gz.at[i - 1], 4 + i, device((z + i) % layers, x, c, y))
            for i in range(1, layers)
        ]

    def add(self, where, got):
        self.kept[where] = (self.kept[where].astype(F32) + got.astype(F32)).astype(BF16)

    def add_across(self):
        z, x, c, y = self.at
        every, a, b = slice(None), slice(0, self.half), slice(self.half, 2 * self.half)

        def add(*where):
            self.add(where, self.got[where])

        add(every, every, 1 - y, a)
        self.first_a().start()
        add(every, 1 - x, every, b)
        self.first_b().start()
        add(every, every, y, a)
        add(every, x, every, b)

    def add_first(self):
        z, x, c, y = self.at
        every, a, b = slice(None), slice(0, self.half), slice(self.half, 2 * self.half)
        self.first_a().wait_recv()
        self.first_a().wait_send()
        self.add((every, 1 - x, y, a), self.a1[:, 1 - x])
        self.second_a().start()
        self.first_b().wait_recv()
        self.first_b().wait_send()
        self.add((every, x, 1 - y, b), self.b1[:, 1 - y])
        self.second_b().start()
        self.add((every, x, y, a), self.a1[:, x])
        self.add((every, x, y, b), self.b1[:, y])

    def add_second(self):
        z, x, c, y = self.at
        every, a, b = slice(None), slice(0, self.half), slice(self.half, 2 * self.half)
        self.second_a().wait_recv()
        self.add((every, x, y, a), self.a2[...])
        self.second_b().wait_recv()
        self.add((every, x, y, b), self.b2[...])
        start(self.along())

    def total(self):
        z, x, c, y = self.at
        wait_recv(self.along())
        value = self.kept[z, x, y].astype(F32)
        for i in range(self.layers - 1):
            value = value + self.gz[i].astype(F32)
        return value

    def drain(self):
        wait_send([self.second_a(), self.second_b(), *self.along()])


def scatter_buffers(rows, cols, layers):
    half = rows // 2
    shapes = [(layers, 2, 2, rows, cols)] * 2 + [(layers, 2, half, cols)] * 2
    shapes += [(layers, half, cols)] * 2 + [(layers - 1, rows, cols)]
    return [pltpu.VMEM(s, BF16) for s in shapes]


def scatter_steps(moves, ready, outs, parts):
    count = len(parts)
    yield

    def due(step, stage):
        lags = [BACK_EARLY if p >= count - 2 else BACK_LATE for p in range(count)]
        return [p for p in range(count) if p + 1 + stage * lags[p] == step]

    for step in range(1, count + 1 + max(3 * BACK_EARLY, 3 * BACK_LATE - 2)):
        for p in due(step, 0):
            ready(p)
            moves[p].add_across()
        for p in due(step, 1):
            moves[p].add_first()
        for p in due(step, 2):
            moves[p].add_second()
        for p in due(step, 3):
            i, (row, rows), (col, cols) = parts[p]
            outs[i][row : row + rows, col : col + cols] = moves[p].total()
        yield


BACK_EARLY, BACK_LATE = 1, 2


def backward_kernel(parts, keep, mix, gain, rate_log, bias_output, hbm, outs, scratch):
    (
        tokens, cotangent, normed_low, narrow, slope, scanned, saved, placed4, taps, mix_t, carry, activated, steep, gated,
        grad_output, w_narrow, w_expand, w_wide, w_output,
    ) = hbm
    layer_out, grad_tokens, *grads = outs
    (
        normed_v, d_normed, d_scanned, conv4, taps_grad, d_pre_narrow, mix_grad_t, sums_wide, sums_small, stage, stage_narrow,
        loads, kept_sems, slot_sems, send, recv, *buffers,
    ) = scratch
    t, e = tokens.shape
    n = mix.shape[0]
    f = activated.shape[1]
    layers = w_output.shape[0]
    z, x, c, y = place()
    moves = [Scatter(buffers[7 * k : 7 * k + 7], send.at[k], recv.at[k]) for k in range(len(parts))]
    used = [0]

    def fetch(source, target):
        copy = pltpu.make_async_copy(source, target, loads.at[used[0]])
        used[0] += 1
        copy.start()
        return copy

    def from_forward(k, core):
        _, rows, cols = parts[k]
        return grad_output.at[pl.ds(0, layers), pl.ds(0, 2), core, pl.ds(0, 2), pl.ds(*rows), pl.ds(*cols)]

    first_own = sum(1 for p in parts if p[0] == 4)
    mine = [pltpu.make_async_copy(from_forward(k, c), moves[k].kept, kept_sems.at[k]) for k in range(first_own)]
    sources = {k: functools.partial(from_forward, k, 1 - c) for k in range(first_own)}
    slots = []

    def ready(k):
        if k < first_own:
            mine[k].wait()
        moves[k].across(sources[k]()).wait_recv()

    def tick(us):
        comm.spend(us, len(sources))

    comm = Progress(scatter_steps(moves, ready, grads, parts), PACE_BACKWARD)

    def slot_for(k):
        if parts[k][0] == 1:
            return lambda: stage_narrow
        at = len(slots) % stage.shape[0]
        if len(slots) >= stage.shape[0]:
            old = slots[-stage.shape[0]]
            moves[old].across(sources[old]()).wait_send()
        slots.append(k)
        return lambda: stage.at[at]

    def put(k, slot, half, value):
        first, second = value[:, :, 0].astype(BF16), value[:, :, 1].astype(BF16)
        moves[k].kept[:, :, half] = jnp.where(c == 0, first, second)
        slot()[:, :, half] = jnp.where(c == 0, second, first)

    def send_across(k, slot):
        sources[k] = slot
        moves[k].across(slot()).start()

    def part_at(array, row, col):
        return next(k for k, p in enumerate(parts) if p[0] == array and p[1][0] == row and p[2][0] == col)

    call_peers(layers)
    hear_peers(layers)
    for k in range(first_own):
        moves[k].across(sources[k]()).start()
    for copy in mine:
        copy.start()
    to_normed = fetch(normed_low, normed_v)
    wide_half, out_half = w_wide.shape[5], w_output.shape[5]
    slab = f // layers

    def wide_parts(d_wide):
        def gate_parts(d_expanded):
            def gating(cotangent_v, weights, d_gated):
                to_cotangent = fetch(cotangent, cotangent_v)

                def fetches(k):
                    cols = pl.ds(k * slab, slab)
                    return [
                        fetch(w_output.at[k], weights.at[k % 2]),
                        fetch(activated.at[:, cols], d_expanded.at[:, cols]),
                        fetch(steep.at[:, cols], d_wide.at[:, cols]),
                    ]

                def multiply(u):
                    k, rows = u // 2, slice(u % 2 * (t // 2), (u % 2 + 1) * (t // 2))
                    d_gated[u % 2] = sum(
                        nt(
                            cotangent_v[rows, h * out_half : (h + 1) * out_half],
                            weights[k % 2, :, :, h].reshape(slab, out_half),
                        )
                        for h in range(2)
                    )

                def gate(u):
                    k, rows = u // 2, slice(u % 2 * (t // 2), (u % 2 + 1) * (t // 2))
                    cols = slice(k * slab, (k + 1) * slab)
                    value = d_gated[u % 2]
                    low = (value * d_expanded[rows, cols].astype(F32)).astype(BF16)
                    d_expanded[rows, cols] = low
                    sums_wide[0:1, cols] = sums(low) if u % 2 == 0 else sums_wide[0:1, cols] + sums(low)
                    low = (value * d_wide[rows, cols].astype(F32)).astype(BF16)
                    d_wide[rows, cols] = low
                    sums_wide[1:2, cols] = sums(low) if u % 2 == 0 else sums_wide[1:2, cols] + sums(low)

                coming = fetches(0)
                to_cotangent.wait()
                for k in range(layers):
                    for copy in coming:
                        copy.wait()
                    multiply(2 * k)
                    if k:
                        gate(2 * k - 1)
                    else:
                        sums_small[0:1, 0:e] = sums(cotangent_v[...])
                    if k + 1 < layers:
                        coming = fetches(k + 1)
                    multiply(2 * k + 1)
                    gate(2 * k)
                    tick(2.8)
                gate(2 * layers - 1)

            pl.run_scoped(
                gating,
                pltpu.VMEM((t, e), BF16),
                pltpu.VMEM((2,) + w_output.shape[1:], BF16),
                pltpu.VMEM((2, t // 2, slab), F32),
            )

            def expanding(weights, scanned_v):
                to_weights, to_scanned = fetch(w_expand, weights), fetch(scanned, scanned_v)
                to_weights.wait()
                lanes = n // 2
                for h in range(2):
                    part = sum(
                        nt(
                            d_expanded[:, k * wide_half : (k + 1) * wide_half],
                            weights[h * layers // 2 : (h + 1) * layers // 2, :, :, k].reshape(lanes, wide_half),
                        )
                        for k in range(2)
                    )
                    d_scanned[:, h * lanes : (h + 1) * lanes] = part.astype(BF16)
                    for g in range(lanes // LANES):
                        conv4[h * (lanes // LANES) + g] = part[:, g * LANES : (g + 1) * LANES]
                    tick(2.4)
                to_scanned.wait()
                for j in range(0, wide_half, TILE):
                    k = part_at(2, 0, j)
                    slot = slot_for(k)
                    for h in range(2):
                        value = tn(scanned_v[...], d_expanded[:, h * wide_half + j : h * wide_half + j + TILE])
                        put(k, slot, h, value.reshape(layers, 2, 2, -1, TILE))
                    send_across(k, slot)
                    tick(1.7)

            pl.run_scoped(expanding, pltpu.VMEM(w_expand.shape, BF16), pltpu.VMEM((t, n), BF16))

        pl.run_scoped(gate_parts, pltpu.VMEM((t, f), BF16))

        def widening(weights, taps_v, placed_v, d_placed):
            to_placed, to_weights, to_taps = fetch(placed4, placed_v), fetch(w_wide, weights), fetch(taps, taps_v)
            groups, blocks = n // LANES, t // BLK
            by_place(conv4, d_placed, blocks)
            to_normed.wait()
            to_placed.wait()
            for j in range(0, wide_half, TILE):
                ks = [k for k, p in enumerate(parts) if p[0] == 3 and p[2][0] == j]
                taken = [slot_for(k) for k in ks]
                for h in range(2):
                    value = tn(normed_v[...], d_wide[:, h * wide_half + j : h * wide_half + j + TILE])
                    g = 2 * (j // TILE) + h
                    if g < groups:
                        correlate_flat(d_placed, placed_v, taps_grad, blocks, g)
                    value = value.reshape(layers, 2, 2, -1, TILE)
                    for k, slot in zip(ks, taken):
                        row, rows = parts[k][1]
                        put(k, slot, h, value[:, :, :, row : row + rows])
                for k, slot in zip(ks, taken):
                    send_across(k, slot)
                tick(4.0)
            to_weights.wait()
            to_taps.wait()
            tiles = wide_half // TILE

            def project(g):
                for q in range(4 * tiles // groups):
                    k = g * (4 * tiles // groups) + q
                    rows = span(lax.rem(k, 2), t // 2)
                    h, j = lax.rem(lax.div(k, 2), 2), lax.div(k, 4)
                    cols = pl.ds(pl.multiple_of(h * wide_half + j * TILE, TILE), TILE)
                    value = nt(d_wide[rows, cols], weights[:, :, :, h, :, span(j, TILE)].reshape(e, TILE))
                    d_normed[rows, :] = d_normed[rows, :] + value
                convolve_back_flat(taps_v, d_placed, conv4, blocks, g)

            d_normed[...] = jnp.zeros(d_normed.shape, F32)
            for g in range(2):
                loop(groups // 2, lambda i: project(g * (groups // 2) + i))
                tick(6.0)

        pl.run_scoped(
            widening, pltpu.VMEM(w_wide.shape, BF16), pltpu.VMEM(taps.shape, F32), pltpu.VMEM(placed4.shape, F32),
            pltpu.VMEM(placed4.shape, F32),
        )

    pl.run_scoped(wide_parts, pltpu.VMEM((t, f), BF16))
    groups = n // LANES
    blocks = t // BLK
    rate = jnp.exp(rate_log[...])

    def scanning(
        narrow_v, slope_v, mix_v, carry_v, adjoint, adjoint_low, product, leave_t,
        overlap, saved_v, d_narrow,
    ):
        coming = [
            fetch(a, b)
            for a, b in (
                (mix_t, mix_v), (carry, carry_v), (narrow, narrow_v), (slope, slope_v),
            )
        ]

        def loading(b):
            return pltpu.make_async_copy(saved.at[b], saved_v.at[b % 2], slot_sems.at[b % 2])

        loading(blocks - 1).start()

        def load(b):
            loading(b).wait()

            @pl.when(b > 0)
            def _():
                loading(b - 1).start()

            return saved_v.at[b % 2]

        for copy in coming:
            copy.wait()
        sums_small[1:2, 0:n] = scan_backward(
            mix[...], rate, lambda b: keep[b], narrow_v, None, d_scanned, None, None, conv4, None, taps_grad, mix_v, carry_v,
            adjoint, adjoint_low, product, leave_t, mix_grad_t, overlap, load, d_narrow, tick, True,
        )
        low = (d_narrow[...] * slope_v[...].astype(F32)).astype(BF16)
        d_pre_narrow[...] = low
        sums_small[2:3, 0:n] = sums(low)

    pl.run_scoped(
        scanning,
        pltpu.VMEM((t, n), BF16), pltpu.VMEM((t, n), BF16), pltpu.VMEM((n, n), F32), pltpu.VMEM((n, LANES), F32),
        pltpu.VMEM((n, n), F32), pltpu.VMEM((n, n), BF16), pltpu.VMEM((n, n), BF16), pltpu.VMEM((n, BLK), BF16),
        pltpu.VMEM((n, LANES), F32), pltpu.VMEM((2, n, n), BF16), pltpu.VMEM((t, n), F32),
    )
    k = part_at(1, 0, 0)
    slot = slot_for(k)
    narrow_half = w_narrow.shape[5]
    for h in range(2):
        value = tn(normed_v[...], d_pre_narrow[:, h * narrow_half : (h + 1) * narrow_half])
        put(k, slot, h, value.reshape(layers, 2, 2, -1, narrow_half))
    send_across(k, slot)
    tick(1.5)

    def ending(tokens_v, cotangent_v, w_narrow_v, gated_v, w_output_v):
        out_v = cotangent_v
        coming = [
            fetch(a, b) for a, b in ((tokens, tokens_v), (w_narrow, w_narrow_v), (cotangent, cotangent_v))
        ]
        later = [fetch(gated, gated_v), fetch(w_output, w_output_v)]
        for copy in coming:
            copy.wait()
        sums_small[3:5, 0:e] = jnp.zeros((2, e), F32)
        tile = t // 4
        writes = []
        for i in range(4):
            rows = slice(i * tile, (i + 1) * tile)
            value = d_normed[rows, :] + sum(
                nt(d_pre_narrow[rows, h * narrow_half : (h + 1) * narrow_half], whole(w_narrow_v, h)) for h in range(2)
            )
            normed, inverse = normalise(tokens_v[rows, :])
            sums_small[3:4, 0:e] += sums(value * normed)
            sums_small[4:5, 0:e] += sums(value)
            scaled = value * gain[...]
            inner = scaled - jnp.mean(scaled, axis=-1, keepdims=True)
            inner = inner - normed * jnp.mean(scaled * normed, axis=-1, keepdims=True)
            d_normed[rows, :] = cotangent_v[rows, :].astype(F32) + inverse * inner
            writes.append(fetch(d_normed.at[rows], grad_tokens.at[rows]))
            tick(1.7)
        k = part_at(0, 0, 0)
        slot = slot_for(k)
        kept = moves[k].kept
        devices = layers * 8
        mix_rows = n // devices
        vectors = [
            sums_small[3:4, 0:e], sums_small[4:5, 0:e], sums_wide[1:2, :], sums_small[2:3, 0:n], sums_small[1:2, 0:n],
            sums_wide[0:1, :], sums_small[0:1, 0:e],
        ]
        packed = [pack(v, devices)[:, None, :] for v in vectors]
        packed.append(jnp.zeros((devices, 16 - len(packed), LANES), F32))
        low = jnp.concatenate(packed, axis=1).astype(BF16).reshape(layers, 2, 2, 2, 16, LANES)
        top = mix_grad_t[...].T.astype(BF16).reshape(layers, 2, 2, 2, mix_rows, n)
        for target, swap in ((kept, False), (slot(), True)):
            for value, rows, cols in (
                (top, slice(0, mix_rows), slice(0, n)), (low, slice(mix_rows, mix_rows + 16), slice(0, LANES)),
            ):
                first, second = value[:, :, 0], value[:, :, 1]
                target[:, :, :, rows, cols] = jnp.where((c == 0) != swap, first, second)
            target[:, :, :, mix_rows : mix_rows + 16, LANES:n] = jnp.zeros((layers, 2, 2, 16, n - LANES), BF16)
        send_across(k, slot)
        tick(2.0)
        for copy in later:
            copy.wait()
        for h in range(2):
            cols = slice(h * out_half, (h + 1) * out_half)
            for i in range(2):
                rows = slice(i * t // 2, (i + 1) * t // 2)
                value = nn(gated_v[rows, :], whole(w_output_v, h)) + bias_output[:, cols]
                out_v[rows, cols] = (value + tokens_v[rows, cols].astype(F32)).astype(BF16)
                comm.spend(2.4)
        writes.append(fetch(out_v, layer_out))
        comm.until(len(parts) + 1 + max(3 * BACK_EARLY, 3 * BACK_LATE - 2))
        for copy in writes:
            copy.wait()

    pl.run_scoped(
        ending,
        pltpu.VMEM((t, e), BF16), pltpu.VMEM((t, e), BF16), pltpu.VMEM(w_narrow.shape, BF16), pltpu.VMEM((t, f), BF16),
        pltpu.VMEM(w_output.shape, BF16),
    )
    sent = slots[-stage.shape[0] :] + [part_at(1, 0, 0)] + list(range(first_own))
    for k in range(len(parts)):
        if k in sent:
            moves[k].across(sources[k]()).wait_send()
        moves[k].drain()


def backward(keep, mix, gain, rate_log, bias_output, hbm, shapes):
    tokens, activated, taps = hbm[0], hbm[11], hbm[8]
    t, e = tokens.shape
    f = activated.shape[1]
    n = mix.shape[0]
    layers = shapes[0][0]
    parts = scatter_parts([s[4:] for s in shapes])
    buffers = [b for _, rows, cols in parts for b in scatter_buffers(rows[1], cols[1], layers)]
    scratch = [
        pltpu.VMEM((t, e), BF16), pltpu.VMEM((t, e), F32), pltpu.VMEM((t, n), BF16),
        pltpu.VMEM((n // LANES, t, LANES), F32), pltpu.VMEM(taps.shape, F32), pltpu.VMEM((t, n), BF16),
        pltpu.VMEM((n, n), F32), pltpu.VMEM((2, f), F32), pltpu.VMEM((8, e), F32), pltpu.VMEM((4, layers, 2, 2, 32, TILE), BF16),
        pltpu.VMEM((layers, 2, 2) + shapes[1][4:], BF16), pltpu.SemaphoreType.DMA((48,)),
        pltpu.SemaphoreType.DMA((len(parts),)), pltpu.SemaphoreType.DMA((2,)),
        pltpu.SemaphoreType.DMA((len(parts), 4 + layers)), pltpu.SemaphoreType.DMA((len(parts), 4 + layers)),
    ] + buffers
    outs = [shape_of(t, e), shape_of(t, e, dtype=F32)] + [shape_of(*s[4:], dtype=F32) for s in shapes]

    def kernel(*refs):
        ins, rest = refs[: 5 + len(hbm)], refs[5 + len(hbm) :]
        backward_kernel(parts, *ins[:5], ins[5:], rest[: len(outs)], rest[len(outs) :])

    return pl.pallas_call(
        kernel,
        out_shape=outs,
        in_specs=[SMEM] + [VMEM] * 4 + [ANY] * len(hbm),
        out_specs=[ANY, ANY] + [VMEM] * len(shapes),
        scratch_shapes=scratch,
        compiler_params=pltpu.CompilerParams(collective_id=1, has_side_effects=True, vmem_limit_bytes=63 << 20),
    )(keep, mix, gain, rate_log, bias_output, *hbm)


def call(kernel, outs, ins, scratch=(), in_specs=None):
    return pl.pallas_call(
        kernel,
        out_shape=outs,
        in_specs=in_specs or [VMEM] * len(ins),
        out_specs=jax.tree.map(lambda _: VMEM, outs),
        scratch_shapes=list(scratch),
        compiler_params=pltpu.CompilerParams(vmem_limit_bytes=58 << 20),
    )(*ins)


def layer(tokens, cotangent, item_lengths, weights, lengths, shapes, parts):
    t, e = tokens.shape
    n = shapes[0][5]
    h = n
    f = lengths[2]
    blocks, groups = t // BLK, h // LANES
    tap_rows = (BLK + 8) * 8
    items = item_lengths.shape[1]
    before = jnp.arange(items)[:, None] < jnp.arange(items)[None, :]
    starts = jnp.sum(jnp.where(before, item_lengths[0][:, None], 0), axis=0)
    firsts = jnp.arange(blocks, dtype=jnp.int32) * BLK
    begins = jnp.any(starts[None, :] == firsts[:, None], axis=1)
    keep = 1.0 - begins.astype(F32)
    by_lane = lambda: shape_of(groups, t, LANES, dtype=F32)
    scratch4 = pltpu.VMEM((groups, t, LANES), F32)
    square = pltpu.VMEM((n, h), F32)
    square_low = pltpu.VMEM((n, h), BF16)
    (
        mix, fields, normed_low, narrow, slope, scanned, saved, placed4, taps, mix_t, carry, activated, steep, gated,
        grad_output, *fulls,
    ) = forward(keep, tokens, cotangent, weights, lengths, shapes, parts)
    w_narrow, w_expand, w_wide, w_output = fulls or weights[1:5]
    gain, _, _, _, rate_log, _, bias_output = fields
    if parts is not None:
        hbm = (
            tokens, cotangent, normed_low, narrow, slope, scanned, saved, placed4, taps, mix_t, carry, activated, steep,
            gated, grad_output, w_narrow, w_expand, w_wide, w_output,
        )
        layer_out, grad_tokens, *grads = backward(keep, mix, gain, rate_log, bias_output, hbm, shapes)
        return layer_out, grad_tokens, grads
    layer_out = jnp.dot(gated, from_blocks(w_output), preferred_element_type=F32) + bias_output
    layer_out = (layer_out + tokens.astype(F32)).astype(BF16)
    row = lambda k: shape_of(1, k, dtype=F32)
    d_pre_wide, d_scanned, d_scanned4, grad_expand, grad_wide, sum_wide, sum_expand, sum_output = call(
        back_kernel,
        [shape_of(t, f), shape_of(t, h), by_lane(), shape_of(*w_expand.shape), shape_of(*w_wide.shape), row(f), row(f), row(e)],
        (cotangent, normed_low, scanned, w_output, w_expand, activated, steep),
        [pltpu.VMEM((t, f), BF16)],
    )
    ins = (keep, mix, rate_log, narrow, placed4, slope, normed_low, d_scanned, d_scanned4, taps, mix_t, carry, saved)
    d_pre_narrow, grad_narrow, mix_grad_t, grad_rate, sum_narrow = call(
        scan_kernel,
        [shape_of(t, h), shape_of(*w_narrow.shape), shape_of(n, h, dtype=F32), row(n), row(h)],
        ins,
        [
            scratch4, scratch4, pltpu.VMEM((groups, tap_rows, LANES), F32), square, square_low, square_low,
            pltpu.VMEM((n, LANES), F32), pltpu.VMEM((t, h), F32), pltpu.VMEM((n, BLK), BF16),
        ],
        [SMEM] + [VMEM] * (len(ins) - 1),
    )
    devices = shapes[0][0] * 8
    grad_tokens, misc_grad = call(
        end_kernel,
        [shape_of(t, e, dtype=F32), shape_of(devices, shapes[0][4], n)],
        (tokens, cotangent, gain, d_pre_wide, d_pre_narrow, w_wide, w_narrow, mix_grad_t,
         sum_wide, sum_narrow, grad_rate, sum_expand, sum_output),
        [pltpu.VMEM((1, e), F32)] * 2,
    )
    misc_grad = misc_grad.reshape(shapes[0])
    return layer_out, grad_tokens, [misc_grad, grad_narrow, grad_expand, grad_wide, grad_output]


VIRTUAL = 4


def block_rows(state_mix, vectors, devices):
    n = state_mix.shape[1]
    rows = [jnp.pad(v.astype(BF16).reshape(devices, 1, -1), ((0, 0), (0, 0), (0, n - v.shape[0] // devices))) for v in vectors]
    rows.append(jnp.zeros((devices, 16 - len(rows), n), BF16))
    return jnp.concatenate([state_mix.astype(BF16).reshape(devices, -1, n)] + rows, axis=1)


def to_blocks(matrix):
    rows, cols = matrix.shape
    return matrix.reshape(VIRTUAL, 2, 2, rows // (4 * VIRTUAL), 2, cols // 2).transpose(0, 1, 2, 4, 3, 5)


def from_blocks(blocks):
    layers, _, _, _, rows, cols = blocks.shape
    return blocks.transpose(0, 1, 2, 4, 3, 5).reshape(layers * 4 * rows, 2 * cols)


def collect(state_mix, vectors, matrices):
    every = ("dp", "fsdp")

    def whole_of(v):
        return lax.all_gather(v.astype(BF16), every, axis=0, tiled=True)

    misc = block_rows(whole_of(state_mix), [whole_of(v) for v in vectors], 8 * VIRTUAL)
    misc = misc.reshape((VIRTUAL, 2, 2, 2) + misc.shape[1:])
    fulls = []
    for m in matrices:
        m = lax.all_gather(m.astype(BF16), "dp", axis=0, tiled=True)
        fulls.append(to_blocks(lax.all_gather(m, "fsdp", axis=1, tiled=True)))
    return [misc] + fulls


def spread(grads, lengths):
    every = ("dp", "fsdp")
    misc, *matrices = grads
    misc = misc.reshape((8 * VIRTUAL,) + misc.shape[4:]).astype(F32)
    n = misc.shape[2]
    mix_rows = n // (8 * VIRTUAL)
    small = [misc[:, :mix_rows].reshape(n, n)]
    small += [misc[:, mix_rows + i, : length // (8 * VIRTUAL)].reshape(length) for i, length in enumerate(lengths)]
    small = [lax.psum_scatter(v, every, scatter_dimension=0, tiled=True) for v in small]
    outs = []
    for m in matrices:
        m = lax.psum_scatter(from_blocks(m).astype(F32), "dp", scatter_dimension=0, tiled=True)
        outs.append(lax.psum_scatter(m, "fsdp", scatter_dimension=1, tiled=True))
    return small[0], small[1:], outs


def fits(dp, fsdp, state_mix, matrices):
    whole_tiles = all(m.shape[0] % 32 == 0 and m.shape[1] % LANES == 0 for m in matrices)
    return dp % 4 == 0 and dp > 4 and fsdp == 2 and state_mix.shape[0] % 16 == 0 and whole_tiles


def shards(
    dp, fsdp, tokens, cotangent, item_lengths, ln_gain, ln_bias, w_wide, bias_wide, w_narrow, bias_narrow, state_mix,
    log_rate, w_expand, bias_expand, w_output, bias_output,
):
    vectors = (ln_gain, ln_bias, bias_wide, bias_narrow, log_rate, bias_expand, bias_output)
    matrices = (w_narrow, w_expand, w_wide, w_output)
    lengths = [v.shape[0] * dp * fsdp for v in vectors]
    if fits(dp, fsdp, state_mix, matrices):
        sizes = [(state_mix.shape[0] + 16, state_mix.shape[1])] + [m.shape for m in matrices]
        weights = [state_mix, *matrices, *(v.reshape(1, -1) for v in vectors)]
        shapes = [(dp // 4, 2, 2, 2) + size for size in sizes]
        parts = gather_parts(sizes)
        layer_out, grad_tokens, grads = layer(tokens, cotangent, item_lengths, weights, lengths, shapes, parts)
        misc_grad, *matrix_grads = grads
        mix_rows = state_mix.shape[0]
        mix_grad = misc_grad[:mix_rows]
        vector_grads = [misc_grad[mix_rows + i, : v.shape[0]] for i, v in enumerate(vectors)]
    else:
        fulls = collect(state_mix, vectors, matrices)
        shapes = [f.shape for f in fulls]
        layer_out, grad_tokens, grads = layer(tokens, cotangent, item_lengths, fulls, lengths, shapes, None)
        mix_grad, vector_grads, matrix_grads = spread(grads, lengths)
    gain_grad, shift_grad, wide_bias_grad, narrow_bias_grad, rate_grad, expand_bias_grad, output_bias_grad = vector_grads
    narrow_grad, expand_grad, wide_grad, output_grad = matrix_grads
    return (
        layer_out, grad_tokens, gain_grad, shift_grad, wide_grad, wide_bias_grad, narrow_grad, narrow_bias_grad,
        mix_grad, rate_grad, expand_grad, expand_bias_grad, output_grad, output_bias_grad,
    )


def solution(mesh):
    every = ("dp", "fsdp")
    matrix, vector, rows = P("dp", "fsdp"), P(every), P(every, None)
    return jax.shard_map(
        functools.partial(shards, mesh.shape["dp"], mesh.shape["fsdp"]),
        mesh=mesh,
        in_specs=(
            rows, rows, rows, vector, vector, matrix, vector, matrix, vector, rows, vector, matrix, vector, matrix, vector,
        ),
        out_specs=(
            rows, rows, vector, vector, matrix, vector, matrix, vector, rows, vector, matrix, vector, matrix, vector,
        ),
        check_vma=False,
    )
```
